512 devices in a mesh: feat: 16 (over y, core), node: 32 (over x, z).
Axes of the slice: x: 4, y: 8, z: 8, core: 2. Of those that a mesh axis runs over, the one named last changes fastest.
Arguments:
- features: bfloat16 [65536, 1024], P('node', 'feat'), may hold values from -6 to 6
- self_rows: int32 [32768], P('node'), may hold values from 0 to 2047
- neighbours: int32 [10, 32768], P(None, 'node'), may hold values from 0 to 65535, as said below
- w_self: bfloat16 [1024, 256], P('feat'), may hold values from -0.25 to 0.25
- w_neigh: bfloat16 [1024, 256], P('feat'), may hold values from -0.5 to 0.5
- cotangent: bfloat16 [32768, 256], P('node'), may hold values from -0.078125 to 0.078125
Outputs:
- hidden: bfloat16 [32768, 256], P(('node', 'feat'))
- grad_self: float32 [1024, 256], P('feat')
- grad_neigh: float32 [1024, 256], P('feat')
The draws below stay inside these ranges and needn't reach their ends.
Inputs may be any that keep to these rules, and one draw needn't show every extreme that they name: `neighbours`: nodes p * 2048 to (p + 1) * 2048 - 1 belong to partition p. Among the 10240 entries of the targets of one partition, every partition is named exactly 3 * 1024 * 10 // 64 times (half of the partitions, the same half for every block) or exactly 1024 * 10 // 64 times (the others).
All inputs are finite; a program needn't handle non-finite values.
Results may differ from the reference program's by a relative error of at most 0.025.
Values may be sent and summed in bfloat16 or wider, within the bound.
A program may use at most 64 MiB of HBM per device.

```python
import jax
import jax.numpy as jnp
import numpy as np
from jax import lax

F = 1024
H = 256
FAN = 10
T_DEV = 1024
NODES_DEV = 2048
TARGETS = 32768
NODES = 65536
N_FEAT = 16
N_NODE = 32


def draw_neighbours(key, part):
    key = jax.random.fold_in(key, 7)
    total = T_DEV * FAN
    middle = total // N_NODE
    counts = [3 * middle // 2 if k < N_NODE // 2 else middle // 2 for k in range(N_NODE)]
    pattern = jnp.asarray(np.repeat(np.arange(N_NODE), counts).astype(np.int32))
    offset = jax.random.randint(jax.random.fold_in(key, 1), (), 0, N_NODE)

    def one_block(index):
        mixed = jax.random.permutation(jax.random.fold_in(jax.random.fold_in(key, 2), index), pattern)
        owner = (mixed + offset) % N_NODE
        local = jax.random.randint(jax.random.fold_in(jax.random.fold_in(key, 3), index), (total,), 0, NODES_DEV)
        return (owner * NODES_DEV + local).reshape(FAN, T_DEV)
    blocks = jax.vmap(one_block)(jnp.arange(N_NODE, dtype=jnp.int32))
    return jnp.transpose(blocks, (1, 0, 2)).reshape(FAN, N_NODE * T_DEV).astype(jnp.int32)


def with_ends(values, key, least, high):
    place = [jax.random.randint(jax.random.fold_in(key, axis), (), 0, length) for axis, length in enumerate(values.shape)]
    longest = values.shape.index(max(values.shape))
    neighbour = place[:longest] + [(place[longest] + 1) % values.shape[longest]] + place[longest + 1:]
    return values.at[tuple(place)].set(least).at[tuple(neighbour)].set(high)


def levels(rng, dims, pieces, least, largest):
    def one(position, blocks):
        draws = jax.random.uniform(jax.random.fold_in(jax.random.fold_in(rng, 6), position), (blocks,), jnp.float32, least / len(pieces), largest / len(pieces))
        return jnp.repeat(jnp.exp(draws), dims[position] // blocks).reshape((-1,) + (1,) * (len(dims) - position - 1))

    loudness = one(*pieces[0])
    for cut in pieces[1:]:
        loudness = loudness * one(*cut)
    return loudness


def normal_values(rng, shape, spread, bound, shards=(), kind=jnp.bfloat16):
    loudness = levels(rng, shape, shards, -0.22, 0.18) if shards else 1.0
    entries = jax.random.normal(rng, shape, jnp.float32) * spread * loudness
    return jnp.minimum(jnp.maximum(entries, -bound), bound).astype(kind)


def setup_inputs(seed: int = 0) -> dict:
    arg_keys = jax.random.split(jax.random.key(seed), 7)
    return {
        "features": normal_values(arg_keys[0], (NODES, F), 1.0, 6.0, ((0, 32), (1, 16))),
        "self_rows": with_ends(jax.random.randint(arg_keys[1], (TARGETS,), 0, NODES_DEV), jax.random.fold_in(arg_keys[1], 1), 0, NODES_DEV - 1).astype(jnp.int32),
        "neighbours": draw_neighbours(jax.random.fold_in(arg_keys[6], 71), 0),
        "w_self": normal_values(arg_keys[3], (F, H), (F // 2) ** -0.5, 0.25, ((0, 16),)),
        "w_neigh": normal_values(arg_keys[4], (F, H), (F // 8) ** -0.5, 0.5, ((0, 16),)),
        "cotangent": normal_values(arg_keys[5], (TARGETS, H), (TARGETS ** -0.5), 0.078125, ((0, 32),)),
    }


def gelu_tanh(value):
    return jax.nn.gelu(value, approximate=True)

def reference(features, self_rows, neighbours, w_self, w_neigh, cotangent):
    width = F // N_FEAT
    w_self_blocks = w_self.reshape(N_FEAT, width, H).astype(jnp.float32)
    w_neigh_blocks = w_neigh.reshape(N_FEAT, width, H).astype(jnp.float32)

    def one_partition(index):
        begin = (index * T_DEV).astype(jnp.int32)
        rows = lax.dynamic_slice_in_dim(self_rows, begin, T_DEV)
        picked = lax.dynamic_slice_in_dim(neighbours, begin, T_DEV, 1)
        own = features[index * NODES_DEV + rows]
        fetched = features[picked.reshape(-1)].reshape(FAN, T_DEV, F)
        neigh_mean = (lax.optimization_barrier(jnp.sum(fetched, axis=0, dtype=jnp.float32)) * (1.0 / FAN)).astype(jnp.bfloat16)
        own_blocks = own.reshape(T_DEV, N_FEAT, width).astype(jnp.float32)
        mean_blocks = neigh_mean.reshape(T_DEV, N_FEAT, width).astype(jnp.float32)
        partial_value = jnp.einsum('tkc,kch->kth', own_blocks, w_self_blocks)
        partial_value = partial_value + jnp.einsum('tkc,kch->kth', mean_blocks, w_neigh_blocks)
        rounded = lax.optimization_barrier(partial_value.astype(jnp.bfloat16))
        pre = lax.optimization_barrier(jnp.sum(rounded.astype(jnp.float32), axis=0))
        grads = lax.dynamic_slice_in_dim(cotangent, begin, T_DEV).astype(jnp.float32)
        acts, backward = jax.vjp(gelu_tanh, pre)
        slope = backward(grads)[0].astype(jnp.bfloat16)
        grad_own = lax.dot_general(own, slope, (((0,), (0,)), ((), ())), preferred_element_type=jnp.float32)
        grad_mean = lax.dot_general(neigh_mean, slope, (((0,), (0,)), ((), ())), preferred_element_type=jnp.float32)
        return (acts.astype(jnp.bfloat16), grad_own, grad_mean)
    outs_all, grad_own_all, grad_mean_all = lax.map(one_partition, jnp.arange(N_NODE, dtype=jnp.int32))
    hidden = outs_all.reshape(TARGETS, H)
    return (hidden, lax.optimization_barrier(jnp.sum(grad_own_all, axis=0)), lax.optimization_barrier(jnp.sum(grad_mean_all, axis=0)))
```

```python
import functools
import math

import jax
import jax.numpy as jnp
from jax import lax
from jax.experimental import pallas as pl
from jax.experimental.pallas import tpu as pltpu
from jax.sharding import PartitionSpec as P

NX, NZ, NY = 4, 8, 8
NODES = NX * NZ
FAN = 10
ROWS = 2048
HALF = ROWS // 2
QUART = HALF // 2
COLS = 64
WIDE = 2 * COLS
HID = 256
SHARE = 64
TGT = NY * SHARE
GROUP = 2 * NX
NZG = NZ // 2
TAB = GROUP * ROWS
MESH = pl.DeviceIdType.MESH
VM = 56 * 2**20

SORT10 = (
    ((0, 8), (1, 9), (2, 7), (3, 5), (4, 6)),
    ((0, 2), (1, 4), (5, 8), (7, 9)),
    ((0, 3), (2, 4), (5, 7), (6, 9)),
    ((0, 1), (3, 6), (8, 9)),
    ((1, 5), (2, 3), (4, 8), (6, 7)),
    ((1, 2), (3, 5), (4, 6), (7, 8)),
    ((2, 3), (4, 5), (6, 7)),
    ((3, 4), (5, 6)),
)


def where_am_i():
    feat, node = lax.axis_index("feat"), lax.axis_index("node")
    return feat // 2, feat % 2, node // NZ, node % NZ


def dev(y, c, x, z):
    return {"feat": y * 2 + c, "node": x * NZ + z}


def remote(src, dst, send, recv, to):
    return pltpu.make_async_remote_copy(
        src_ref=src, dst_ref=dst, send_sem=send, recv_sem=recv, device_id=to, device_id_type=MESH
    )


def gather_kernel(feat, nb, ws, wn, tab, idx, cnt, wf, other, nbs, s_x, r_x, s_t, r_t, s_n, r_n, s_w, r_w, s_f, r_f):
    y, c, x, z = where_am_i()
    zl, zh = z % 2, z // 2
    xr, xl, zp = (x + 1) % NX, (x + NX - 1) % NX, z + 1 - 2 * zl
    right, left, over = dev(y, c, xr, z), dev(y, c, xl, z), dev(y, c, x, zp)
    partner = dev(y, 1 - c, x, z)
    barrier = pltpu.get_barrier_semaphore()
    for to in (right, left, over, partner):
        pl.semaphore_signal(barrier, inc=1, device_id=to, device_id_type=MESH)
    for d in range(1, NZG):
        pl.semaphore_signal(barrier, inc=1, device_id=dev(y, c, x, (z + 2 * d) % NZ), device_id_type=MESH)
    for d in range(1, NY):
        pl.semaphore_signal(barrier, inc=1, device_id=dev((y + d) % NY, c, x, z), device_id_type=MESH)

    k = y * 2 + c
    wf[k, 0] = ws[...]
    wf[k, 1] = wn[...]
    mine = []
    for b in range(NY):
        lo = nb[:, b * 128 : b * 128 + 64]
        hi = nb[:, b * 128 + 64 : b * 128 + 128]
        mine.append(jnp.where(c == 0, lo, hi))
    nbs[zh] = jnp.concatenate(mine, axis=1)

    pl.semaphore_wait(barrier, 4 + (NZG - 1) + (NY - 1))

    give = pl.multiple_of((1 - c) * HALF, HALF)
    keep = pl.multiple_of(c * HALF, HALF)
    swap = remote(feat.at[pl.ds(give, HALF)], other, s_x, r_x, partner)
    swap.start()
    for d in range(1, NZG):
        remote(nbs.at[zh], nbs.at[zh], s_n.at[d], r_n.at[d], dev(y, c, x, (z + 2 * d) % NZ)).start()
    for d in range(1, NY):
        remote(wf.at[k], wf.at[k], s_w.at[d], r_w.at[d], dev((y + d) % NY, c, x, z)).start()
    remote(wf.at[k], wf.at[k], s_f.at[0], r_f.at[0], partner).start()
    swap.wait_recv()
    own = x * 2 + zl

    def widen(i, _):
        at = pl.multiple_of(i * 128, 128)
        a = feat[pl.ds(keep + at, 128), :]
        b = other[pl.ds(at, 128), :]
        tab[own, c, pl.ds(at, 128), :] = jnp.where(
            c == 0, jnp.concatenate([a, b], axis=1), jnp.concatenate([b, a], axis=1)
        )
        return 0

    lax.fori_loop(0, HALF // 128, widen, 0)

    slot = lambda i, zz: i * 2 + zz
    zo = 1 - zl
    whole = lambda i, zz: tab.at[slot(i, zz), c]
    part = lambda i, zz, h: tab.at[slot(i, zz), c, pl.ds(h * QUART, QUART)]
    far = (x + 2) % NX
    sends = []

    def go(m, ref, to):
        copy = remote(ref, ref, s_t.at[m], r_t.at[m], to)
        copy.start()
        sends.append(copy)

    def come(m, ref):
        remote(ref, ref, s_t.at[m], r_t.at[m], partner).wait_recv()

    go(0, whole(x, zl), right)
    go(1, whole(x, zl), left)
    go(2, whole(x, zl), over)
    go(9, whole(x, zl), partner)
    come(0, whole(xl, zl))
    go(3, part(xl, zl, 0), right)
    go(10, whole(xl, zl), partner)
    come(1, whole(xr, zl))
    go(4, part(xr, zl, 1), left)
    go(11, whole(xr, zl), partner)
    come(2, whole(x, zo))
    go(5, whole(x, zo), right)
    go(6, whole(x, zo), left)
    go(12, whole(x, zo), partner)
    come(3, part(far, zl, 0))
    go(7, part(far, zl, 0), over)
    go(13, part(far, zl, 0), partner)
    come(4, part(far, zl, 1))
    go(8, part(far, zl, 1), over)
    go(14, part(far, zl, 1), partner)

    for d in range(1, NZG):
        at = (zh + NZG - d) % NZG
        remote(nbs.at[at], nbs.at[at], s_n.at[d], r_n.at[d], partner).wait_recv()
    wires = []
    for f in range(FAN):
        n = jnp.concatenate([nbs[g, f : f + 1, :] for g in range(NZG)], axis=0)
        part_of = n >> 11
        inside = ((part_of & 7) >> 1) == zh
        row = ((((part_of >> 3) << 1) | (part_of & 1)) << 11) | (n & (ROWS - 1))
        wires.append(jnp.where(inside, row, TAB))
    for layer in SORT10:
        for a, b in layer:
            wires[a], wires[b] = jnp.minimum(wires[a], wires[b]), jnp.maximum(wires[a], wires[b])
    count = sum((w < TAB).astype(jnp.int32) for w in wires)
    most = count[:, :SHARE]
    for b in range(1, NY):
        most = jnp.maximum(most, count[:, b * SHARE : (b + 1) * SHARE])
    cnt[...] = most
    for f in range(FAN):
        packed = wires[f][:, : TGT // 2] | (wires[f][:, TGT // 2 :] << 16)
        for g in range(NZG):
            idx[g * FAN + f : g * FAN + f + 1, :] = packed[g : g + 1, :]

    for d in range(1, NY):
        at = ((y + NY - d) % NY) * 2 + c
        remote(wf.at[at], wf.at[at], s_w.at[d], r_w.at[d], partner).wait_recv()
        remote(wf.at[at], wf.at[at], s_f.at[d], r_f.at[d], partner).start()

    come(5, whole(xl, zo))
    go(15, whole(xl, zo), partner)
    come(6, whole(xr, zo))
    go(16, whole(xr, zo), partner)
    come(7, part(far, zo, 0))
    go(17, part(far, zo, 0), partner)
    come(8, part(far, zo, 1))
    go(18, part(far, zo, 1), partner)

    o = 1 - c
    owhole = lambda i, zz: tab.at[slot(i, zz), o]
    opart = lambda i, zz, h: tab.at[slot(i, zz), o, pl.ds(h * QUART, QUART)]
    come(9, owhole(x, zl))
    come(10, owhole(xl, zl))
    come(11, owhole(xr, zl))
    come(12, owhole(x, zo))
    come(13, opart(far, zl, 0))
    come(14, opart(far, zl, 1))
    come(15, owhole(xl, zo))
    come(16, owhole(xr, zo))
    come(17, opart(far, zo, 0))
    come(18, opart(far, zo, 1))
    for d in range(NY):
        at = ((y + NY - d) % NY) * 2 + 1 - c
        remote(wf.at[at], wf.at[at], s_f.at[d], r_f.at[d], partner).wait_recv()

    swap.wait_send()
    for copy in sends:
        copy.wait_send()
    for d in range(1, NZG):
        remote(nbs.at[zh], nbs.at[zh], s_n.at[d], r_n.at[d], partner).wait_send()
    for d in range(1, NY):
        remote(wf.at[k], wf.at[k], s_w.at[d], r_w.at[d], partner).wait_send()
    for d in range(NY):
        at = ((y + NY - d) % NY) * 2 + c
        remote(wf.at[at], wf.at[at], s_f.at[d], r_f.at[d], partner).wait_send()


def lookup_kernel(cnt, idx, rows, tab, psum, own, wide, acc):
    _, c, x, z = where_am_i()

    def conv(i, _):
        at = pl.multiple_of(i * 128, 128)
        wide[pl.ds(at, 128), :] = tab[pl.ds(at, 128), :].astype(jnp.float32)
        return 0

    lax.fori_loop(0, TAB // 128, conv, 0)
    wide[pl.ds(TAB, 8), :] = jnp.zeros((8, WIDE), jnp.float32)

    def eight(line, i):
        rows8 = []
        upper = []
        for b in range(NY // 2):
            v = idx[line, b * SHARE + i]
            rows8.append(wide[pl.ds(v & 0xFFFF, 1), :])
            upper.append(wide[pl.ds(v >> 16, 1), :])
        return jnp.concatenate(rows8 + upper, axis=0)

    for g in range(NZG):

        def chunk(i, _):
            total = eight(g * FAN, i) + eight(g * FAN + 1, i) + eight(g * FAN + 2, i)
            total = lax.fori_loop(3, cnt[g, i], lambda f, t: t + eight(g * FAN + f, i), total)
            acc[pl.ds(pl.multiple_of(i * NY, NY), NY), :] = total
            return 0

        lax.fori_loop(0, SHARE, chunk, 0)
        for b in range(NY):
            psum[g, b * SHARE : (b + 1) * SHARE, :] = acc[pl.ds(b, SHARE, stride=NY), :].astype(jnp.bfloat16)

    base = (x * 2 + z % 2) * ROWS

    def mine(i, _):
        got = [wide[pl.ds(base + rows[b * 128 + c * 64 + i], 1), :] for b in range(NY)]
        acc[pl.ds(pl.multiple_of(i * NY, NY), NY), :] = jnp.concatenate(got, axis=0)
        return 0

    lax.fori_loop(0, SHARE, mine, 0)
    for b in range(NY):
        own[b * SHARE : (b + 1) * SHARE, :] = acc[pl.ds(b, SHARE, stride=NY), :].astype(jnp.bfloat16)


ROOT = math.sqrt(2.0 / math.pi)


def layer_kernel(
    psum, own, wf, cot, hidden, gself, gneigh,
    rz, both, abuf, slopes, gout, gin, gsend, grecv, gred, gfull,
    s_z, r_z, s_o, r_o, s_m, r_m, s_s, r_s, s_c, r_c, s_r, r_r, s_g, r_g,
):
    y, c, x, z = where_am_i()
    zl, zh = z % 2, z // 2
    node = x * NZ + z
    partner = dev(y, 1 - c, x, z)
    at_y = lambda d: dev((y + d) % NY, c, x, z)
    feat_id = y * 2 + c
    at_node = lambda q: {"feat": feat_id, "node": q}
    barrier = pltpu.get_barrier_semaphore()
    pl.semaphore_signal(barrier, inc=1, device_id=partner, device_id_type=MESH)
    for d in range(1, NY):
        pl.semaphore_signal(barrier, inc=1, device_id=at_y(d), device_id_type=MESH)

    def greet(d, _):
        pl.semaphore_signal(barrier, inc=1, device_id=at_node((node + d) % NODES), device_id_type=MESH)
        return 0

    lax.fori_loop(1, NODES, greet, 0)
    pl.semaphore_wait(barrier, 1 + NY - 1 + NODES - 1)

    for d in range(1, NZG):
        to = dev(y, c, x, (z + 2 * d) % NZ)
        remote(psum.at[(zh + d) % NZG], rz.at[d - 1], s_z.at[d], r_z.at[d], to).start()

    def block(ref, b):
        return ref.at[pl.ds(pl.multiple_of(b * SHARE, SHARE), SHARE)]

    for d in range(1, NY):
        remote(block(own, (y + d) % NY), abuf.at[y, 0], s_o.at[d], r_o.at[d], at_y(d)).start()
    abuf[y, 0] = own[pl.ds(pl.multiple_of(y * SHARE, SHARE), SHARE), :]
    both[0] = own[...]
    for d in range(1, NZG):
        remote(psum.at[zh], rz.at[d - 1], s_z.at[d], r_z.at[d], partner).wait_recv()
    total = psum[zh].astype(jnp.float32)
    for d in range(NZG - 1):
        total = total + rz[d].astype(jnp.float32)
    both[1] = (total * (1.0 / FAN)).astype(jnp.bfloat16)
    for d in range(1, NY):
        remote(block(both.at[1], (y + d) % NY), abuf.at[y, 1], s_m.at[d], r_m.at[d], at_y(d)).start()
    abuf[y, 1] = both[1, pl.ds(pl.multiple_of(y * SHARE, SHARE), SHARE), :]
    for d in range(1, NY):
        src = (y + NY - d) % NY
        remote(abuf.at[src, 0], abuf.at[src, 0], s_o.at[d], r_o.at[d], partner).wait_recv()
        remote(abuf.at[src, 1], abuf.at[src, 1], s_m.at[d], r_m.at[d], partner).wait_recv()
    pre = jnp.zeros((SHARE, HID), jnp.float32)
    for b in range(NY):
        for s in range(2):
            w = jnp.concatenate([wf[2 * b, s], wf[2 * b + 1, s]], axis=0)
            pre = pre + jnp.dot(abuf[b, s], w, preferred_element_type=jnp.float32)
    square = pre * pre
    th = jnp.tanh(ROOT * (pre + 0.044715 * (square * pre)))
    half = 0.5 * (1.0 + th)
    hidden[...] = (pre * half).astype(jnp.bfloat16)
    dydx = half + 0.5 * pre * (1.0 - th * th) * (ROOT * (1.0 + 3.0 * 0.044715 * square))
    grads = cot[pl.ds(pl.multiple_of(feat_id * SHARE, SHARE), SHARE), :].astype(jnp.float32)
    slopes[y] = (grads * dydx).astype(jnp.bfloat16)
    for d in range(1, NY):
        remote(slopes.at[y], slopes.at[y], s_s.at[d], r_s.at[d], at_y(d)).start()
    turned = [jnp.transpose(both[s]) for s in range(2)]
    for d in range(1, NY):
        src = (y + NY - d) % NY
        remote(slopes.at[src], slopes.at[src], s_s.at[d], r_s.at[d], partner).wait_recv()
    slope = slopes[...].reshape(TGT, HID)
    keep = pl.multiple_of(c * COLS, COLS)
    give = pl.multiple_of((1 - c) * COLS, COLS)
    whole = [jnp.dot(turned[s], slope, preferred_element_type=jnp.float32) for s in range(2)]
    for s in range(2):
        gout[s] = jnp.where(c == 0, whole[s][COLS:], whole[s][:COLS]).astype(jnp.bfloat16)
    swap = remote(gout, gin, s_c, r_c, partner)
    swap.start()
    stay = [jnp.where(c == 0, whole[s][:COLS], whole[s][COLS:]) for s in range(2)]
    swap.wait_recv()
    for s in range(2):
        mine = stay[s] + gin[s].astype(jnp.float32)
        for r in range(8):
            for h in range(2):
                gsend[s * 16 + r * 2 + h] = mine[r * 8 : r * 8 + 8, h * 128 : h * 128 + 128]

    def scatter(d, _):
        to = (node + d) % NODES
        remote(gsend.at[to], grecv.at[d], s_r.at[d], r_r.at[d], at_node(to)).start()
        return 0

    lax.fori_loop(1, NODES, scatter, 0)

    def collect(d, t):
        remote(gsend.at[0], grecv.at[d], s_r.at[d], r_r.at[d], partner).wait_recv()
        return t + grecv[d]

    gfull[node] = lax.fori_loop(1, NODES, collect, gsend[node])

    def spread(d, _):
        remote(gfull.at[node], gfull.at[node], s_g.at[d], r_g.at[d], at_node((node + d) % NODES)).start()
        return 0

    lax.fori_loop(1, NODES, spread, 0)

    def arrive(d, _):
        src = (node + NODES - d) % NODES
        remote(gfull.at[src], gfull.at[src], s_g.at[d], r_g.at[d], partner).wait_recv()
        return 0

    lax.fori_loop(1, NODES, arrive, 0)
    for s, out in enumerate((gself, gneigh)):
        for r in range(8):
            for h in range(2):
                out[r * 8 : r * 8 + 8, h * 128 : h * 128 + 128] = gfull[s * 16 + r * 2 + h]

    for d in range(1, NZG):
        remote(psum.at[zh], rz.at[d - 1], s_z.at[d], r_z.at[d], partner).wait_send()
    for d in range(1, NY):
        remote(abuf.at[y, 0], abuf.at[y, 0], s_o.at[d], r_o.at[d], partner).wait_send()
        remote(abuf.at[y, 1], abuf.at[y, 1], s_m.at[d], r_m.at[d], partner).wait_send()
        remote(slopes.at[y], slopes.at[y], s_s.at[d], r_s.at[d], partner).wait_send()
    swap.wait_send()

    def drain(d, _):
        remote(gsend.at[0], grecv.at[d], s_r.at[d], r_r.at[d], partner).wait_send()
        remote(gfull.at[node], gfull.at[node], s_g.at[d], r_g.at[d], partner).wait_send()
        return 0

    lax.fori_loop(1, NODES, drain, 0)


VMEM = pl.BlockSpec(memory_space=pltpu.VMEM)
SMEM = pl.BlockSpec(memory_space=pltpu.SMEM)
DMA = pltpu.SemaphoreType.DMA


def on_device(features, self_rows, neighbours, w_self, w_neigh, cotangent):
    bf, f32, i32 = jnp.bfloat16, jnp.float32, jnp.int32
    shape = jax.ShapeDtypeStruct
    tab, idx, cnt, wf = pl.pallas_call(
        gather_kernel,
        out_shape=[
            shape((GROUP, 2, HALF, WIDE), bf),
            shape((NZG * FAN, TGT // 2), i32),
            shape((NZG, SHARE), i32),
            shape((2 * NY, 2, COLS, HID), bf),
        ],
        in_specs=[VMEM] * 4,
        out_specs=[VMEM] * 4,
        scratch_shapes=[
            pltpu.VMEM((HALF, COLS), bf),
            pltpu.VMEM((NZG, FAN, TGT), i32),
            DMA, DMA, DMA((19,)), DMA((19,)), DMA((NZG,)), DMA((NZG,)),
            DMA((NY,)), DMA((NY,)), DMA((NY,)), DMA((NY,)),
        ],
        compiler_params=pltpu.CompilerParams(collective_id=0, has_side_effects=True, vmem_limit_bytes=VM),
        name="gather_rows",
    )(features, neighbours, w_self, w_neigh)
    psum, own = pl.pallas_call(
        lookup_kernel,
        out_shape=[shape((NZG, TGT, WIDE), bf), shape((TGT, WIDE), bf)],
        in_specs=[SMEM, SMEM, SMEM, VMEM],
        out_specs=[VMEM] * 2,
        scratch_shapes=[pltpu.VMEM((TAB + 8, WIDE), f32), pltpu.VMEM((TGT, WIDE), f32)],
        compiler_params=pltpu.CompilerParams(vmem_limit_bytes=VM),
        name="lookup_rows",
    )(cnt, idx, self_rows, tab.reshape(TAB, WIDE))
    return pl.pallas_call(
        layer_kernel,
        out_shape=[shape((SHARE, HID), bf), shape((COLS, HID), f32), shape((COLS, HID), f32)],
        in_specs=[VMEM] * 4,
        out_specs=[VMEM] * 3,
        scratch_shapes=[
            pltpu.VMEM((NZG - 1, TGT, WIDE), bf),
            pltpu.VMEM((2, TGT, WIDE), bf),
            pltpu.VMEM((NY, 2, SHARE, WIDE), bf),
            pltpu.VMEM((NY, SHARE, HID), bf),
            pltpu.VMEM((2, COLS, HID), bf),
            pltpu.VMEM((2, COLS, HID), bf),
            pltpu.VMEM((NODES, 8, 128), f32),
            pltpu.VMEM((NODES, 8, 128), f32),
            pltpu.VMEM((8, 128), f32),
            pltpu.VMEM((NODES, 8, 128), f32),
            DMA((NZG,)), DMA((NZG,)),
            DMA((NY,)), DMA((NY,)), DMA((NY,)), DMA((NY,)), DMA((NY,)), DMA((NY,)),
            DMA, DMA,
            DMA((NODES,)), DMA((NODES,)), DMA((NODES,)), DMA((NODES,)),
        ],
        compiler_params=pltpu.CompilerParams(collective_id=1, has_side_effects=True, vmem_limit_bytes=VM),
        name="layer",
    )(psum, own, wf, cotangent)


def solution(mesh):
    return jax.shard_map(
        on_device,
        mesh=mesh,
        in_specs=(
            P("node", "feat"),
            P("node"),
            P(None, "node"),
            P("feat", None),
            P("feat", None),
            P("node", None),
        ),
        out_specs=(P(("node", "feat"), None), P("feat", None), P("feat", None)),
        check_vma=False,
    )
```

```python
import math

import jax
import jax.numpy as jnp
from jax import lax
from jax.experimental import pallas as pl
from jax.experimental.pallas import tpu as pltpu
from jax.sharding import PartitionSpec as P

NX, NZ, NY = 4, 8, 8
FAN = 10
PAIR = FAN // 2
ROWS = 2048
HALF = ROWS // 2
UNIT = HALF // 2
COLS = 64
WIDE = 2 * COLS
HID = 256
SHARE = 64
TGT = NY * SHARE
GROUP = 2 * NX
NZG = NZ // 2
TAB = GROUP * ROWS
QROW = COLS // NX
NS = 1
RB = SHARE // NS
MESH = pl.DeviceIdType.MESH
ROOT = math.sqrt(2.0 / math.pi)
BF, F32, I32 = jnp.bfloat16, jnp.float32, jnp.int32


def kernel(
    feat, nb, rows, ws, wn, cot, hidden, gself, gneigh,
    pieces, tab, wide, nbs, lists, idx, wf, own, theirs, stage, pin, mine, slopes, means,
    gsend, gx, gz, gq,
    s_x, r_x, s_t, r_t, s_n, r_n, s_w, r_w, s_f, r_f, s_o, r_o, s_p, r_p, s_s, r_s, s_m, r_m,
    s_gx, r_gx, s_gz, r_gz, s_gq, r_gq, s_idx,
):
    f_id, n_id = lax.axis_index("feat"), lax.axis_index("node")
    y, c, x, z = f_id // 2, f_id % 2, n_id // NZ, n_id % NZ
    zl, zh = z % 2, z // 2

    def dev(dy, dc, dx, dz):
        core = 1 - c if dc else c
        return {"feat": ((y + dy) % NY) * 2 + core, "node": ((x + dx) % NX) * NZ + (z + dz) % NZ}

    partner = dev(0, 1, 0, 0)
    right, left = dev(0, 0, 1, 0), dev(0, 0, NX - 1, 0)
    over = {"feat": f_id, "node": x * NZ + z + 1 - 2 * zl}

    def remote(src, dst, send, recv, to):
        return pltpu.make_async_remote_copy(
            src_ref=src, dst_ref=dst, send_sem=send, recv_sem=recv, device_id=to, device_id_type=MESH
        )

    def arrived(ref, recv):
        remote(ref, ref, recv, recv, partner).wait_recv()

    def left_here(ref, send):
        remote(ref, ref, send, send, partner).wait_send()

    barrier = pltpu.get_barrier_semaphore()
    friends = [partner]
    friends += [dev(0, 0, 0, d) for d in range(1, NZ)]
    friends += [dev(0, dc, d, 0) for d in range(1, NX) for dc in range(2)]
    friends += [dev(e, 0, 0, 2 * d) for d in range(NZG) for e in range(1, NY)]
    for to in friends:
        pl.semaphore_signal(barrier, inc=1, device_id=to, device_id_type=MESH)

    wf[f_id, 0] = ws[...]
    wf[f_id, 1] = wn[...]
    cuts = []
    for b in range(NY):
        lo = nb[:, b * 128 : b * 128 + 64]
        hi = nb[:, b * 128 + 64 : b * 128 + 128]
        cuts.append(jnp.where(c == 0, lo, hi))
    nbs[zh] = jnp.concatenate(cuts, axis=1)
    give = pl.multiple_of((1 - c) * HALF, HALF)
    keep = pl.multiple_of(c * HALF, HALF)
    pieces[c] = feat[:, pl.ds(keep, HALF)]

    pl.semaphore_wait(barrier, len(friends))

    swap = remote(feat.at[:, pl.ds(give, HALF)], pieces.at[c], s_x, r_x, partner)
    swap.start()
    for d in range(1, NZG):
        remote(nbs.at[zh], nbs.at[zh], s_n.at[d], r_n.at[d], dev(0, 0, 0, 2 * d)).start()
    arrived(pieces.at[1 - c], r_x)
    home = x * 2 + zl

    def turn(i, _):
        at = pl.multiple_of(i * 256, 256)
        block = pieces[:, :, pl.ds(at, 256)].reshape(WIDE, 256)
        tab[home, c, pl.ds(at, 256), :] = jnp.transpose(block)
        return 0

    lax.fori_loop(0, HALF // 256, turn, 0)

    xr, xl, far, zo = (x + 1) % NX, (x + NX - 1) % NX, (x + 2) % NX, 1 - zl

    def unit(i, zz, h, core):
        return tab.at[i * 2 + zz, core, pl.ds(h * UNIT, UNIT)]

    def widen(i, zz, h, core):
        base = ((i * 2 + zz) * 2 + core) * HALF + h * UNIT

        def step(k, _):
            at = pl.multiple_of(k * 128, 128)
            piece = tab[i * 2 + zz, core, pl.ds(h * UNIT + at, 128), :]
            wide[pl.ds(pl.multiple_of(base + at, 128), 128), :] = piece.astype(F32)
            return 0

        lax.fori_loop(0, UNIT // 128, step, 0)

    sent = []

    def go(m, i, zz, h, to):
        ref = unit(i, zz, h, c)
        remote(ref, ref, s_t.at[m], r_t.at[m], to).start()
        sent.append((ref, s_t.at[m]))

    passed = []

    def pass_on(i, zz, h):
        m = 14 + len(passed)
        go(m, i, zz, h, partner)
        passed.append((m, i, zz, h))

    def come(m, i, zz, h):
        arrived(unit(i, zz, h, c), r_t.at[m])

    go(0, x, zl, 0, right)
    go(3, x, zl, 1, left)
    go(4, x, zl, 0, over)
    go(1, x, zl, 1, right)
    go(2, x, zl, 0, left)
    go(5, x, zl, 1, over)
    pass_on(x, zl, 0)
    pass_on(x, zl, 1)
    for d in range(1, NY):
        remote(wf.at[f_id], wf.at[f_id], s_w.at[d], r_w.at[d], dev(d, 0, 0, 0)).start()
    remote(wf.at[f_id], wf.at[f_id], s_f.at[0], r_f.at[0], partner).start()
    widen(x, zl, 0, c)
    widen(x, zl, 1, c)

    for d in range(1, NZG):
        at = (zh + NZG - d) % NZG
        arrived(nbs.at[at], r_n.at[d])
    for g in range(NZG):
        n = nbs[g]
        part_of = n >> 11
        inside = ((part_of & 7) >> 1) == zh
        row = ((((part_of >> 3) << 1) | (part_of & 1)) << 11) | (n & (ROWS - 1))
        row = jnp.where(inside, row, TAB)
        lists[g * 8 : g * 8 + PAIR, :] = row[:PAIR] | (row[PAIR:] << 16)
    to_scalar = pltpu.make_async_copy(lists, idx, s_idx)
    to_scalar.start()

    arrived(unit(x, zl, 0, 1 - c), r_t.at[14])
    widen(x, zl, 0, 1 - c)
    arrived(unit(x, zl, 1, 1 - c), r_t.at[15])
    widen(x, zl, 1, 1 - c)

    def fetch_own(k, _):
        got = [
            wide[pl.ds(home * ROWS + rows[(k // 8) * 128 + c * SHARE + (k % 8) * 8 + u], 1), :] for u in range(8)
        ]
        own[pl.ds(pl.multiple_of(k * 8, 8), 8), :] = jnp.concatenate(got, axis=0)
        return 0

    come(0, xl, zl, 0)
    go(6, xl, zl, 0, right)
    pass_on(xl, zl, 0)
    come(3, xr, zl, 1)
    go(7, xr, zl, 1, left)
    pass_on(xr, zl, 1)
    come(4, x, zo, 0)
    go(8, x, zo, 0, right)
    go(9, x, zo, 0, left)
    pass_on(x, zo, 0)
    widen(xl, zl, 0, c)
    widen(xr, zl, 1, c)
    come(1, xl, zl, 1)
    pass_on(xl, zl, 1)
    come(2, xr, zl, 0)
    pass_on(xr, zl, 0)
    come(5, x, zo, 1)
    go(10, x, zo, 1, right)
    go(11, x, zo, 1, left)
    pass_on(x, zo, 1)
    lax.fori_loop(0, TGT // 8, fetch_own, 0)
    means[NS] = own[...].astype(BF).reshape(NY, SHARE, WIDE)
    theirs[y] = means[NS, y]
    for e in range(1, NY):
        remote(means.at[NS, (y + e) % NY], theirs.at[y], s_o.at[e], r_o.at[e], dev(e, 0, 0, 0)).start()
    widen(x, zo, 0, c)
    widen(xl, zl, 1, c)
    widen(xr, zl, 0, c)
    widen(x, zo, 1, c)
    come(6, far, zl, 0)
    go(12, far, zl, 0, over)
    pass_on(far, zl, 0)
    come(7, far, zl, 1)
    go(13, far, zl, 1, over)
    pass_on(far, zl, 1)
    for d in range(1, NY):
        at = ((y + NY - d) % NY) * 2 + c
        arrived(wf.at[at], r_w.at[d])
        remote(wf.at[at], wf.at[at], s_f.at[d], r_f.at[d], partner).start()
    widen(far, zl, 0, c)
    widen(far, zl, 1, c)
    come(8, xl, zo, 0)
    pass_on(xl, zo, 0)
    come(9, xr, zo, 0)
    pass_on(xr, zo, 0)
    widen(xl, zo, 0, c)
    widen(xr, zo, 0, c)
    come(10, xl, zo, 1)
    pass_on(xl, zo, 1)
    come(11, xr, zo, 1)
    pass_on(xr, zo, 1)
    come(12, far, zo, 0)
    pass_on(far, zo, 0)
    come(13, far, zo, 1)
    pass_on(far, zo, 1)
    widen(xl, zo, 1, c)
    widen(xr, zo, 1, c)
    widen(far, zo, 0, c)
    widen(far, zo, 1, c)
    for m, i, zz, h in passed[2:]:
        arrived(unit(i, zz, h, 1 - c), r_t.at[m])
        widen(i, zz, h, 1 - c)
    wide[pl.ds(TAB, 8), :] = jnp.zeros((8, WIDE), F32)
    to_scalar.wait()

    def block(g, b, s, put):
        def eight(k, _):
            out = []
            for u in range(8):
                t = b * SHARE + s * RB + k * 8 + u
                v = idx[g * 8, t]
                total = wide[pl.ds(v & 0xFFFF, 1), :] + wide[pl.ds(v >> 16, 1), :]
                for j in range(1, PAIR):
                    v = idx[g * 8 + j, t]
                    total = total + wide[pl.ds(v & 0xFFFF, 1), :]
                    total = total + wide[pl.ds(v >> 16, 1), :]
                out.append(total)
            own[pl.ds(pl.multiple_of(k * 8, 8), 8), :] = jnp.concatenate(out, axis=0)
            return 0

        lax.fori_loop(0, RB // 8, eight, 0)
        put[...] = own[pl.ds(0, RB), :].astype(BF)

    def plane(s, d):
        g = (zh + d) % NZG

        def one(e, _):
            at = (s * NZG + d) * NY + e
            block(g, (y + e) % NY, s, stage.at[at])
            remote(stage.at[at], pin.at[at], s_p.at[at], r_p.at[at], dev(e, 0, 0, 2 * d)).start()
            return 0

        lax.fori_loop(1 if d == 0 else 0, NY, one, 0)
        if d == 0:
            block(g, y, s, pin.at[s * NZG * NY])

    def activate(s):
        pre = jnp.zeros((RB, HID), F32)
        for e in range(NY):
            src = (y + NY - e) % NY
            total = jnp.zeros((RB, WIDE), F32)
            for d in range(NZG):
                at = (s * NZG + d) * NY + e
                if d or e:
                    arrived(pin.at[at], r_p.at[at])
                total = total + pin[at].astype(F32)
            mean = (total * (1.0 / FAN)).astype(BF)
            if e:
                mine[s * NY + e] = mean
                to = dev(NY - e, 0, 0, 0)
                remote(mine.at[s * NY + e], means.at[s, y], s_m.at[s * NY + e], r_m.at[s * NY + e], to).start()
            else:
                means[s, y] = mean
            w_own = jnp.concatenate([wf[2 * src, 0], wf[2 * src + 1, 0]], axis=0)
            w_mean = jnp.concatenate([wf[2 * src, 1], wf[2 * src + 1, 1]], axis=0)
            rows_own = theirs[src, s * RB : (s + 1) * RB, :]
            pre = pre + jnp.dot(rows_own, w_own, preferred_element_type=F32)
            pre = pre + jnp.dot(mean, w_mean, preferred_element_type=F32)
        square = pre * pre
        th = jnp.tanh(ROOT * (pre + 0.044715 * (square * pre)))
        half = 0.5 * (1.0 + th)
        dydx = half + 0.5 * pre * (1.0 - th * th) * (ROOT * (1.0 + 3.0 * 0.044715 * square))
        first = pl.multiple_of(f_id * SHARE + s * RB, RB)
        slopes[s, y] = (cot[pl.ds(first, RB), :].astype(F32) * dydx).astype(BF)
        for e in range(1, NY):
            at = s * NY + e
            remote(slopes.at[s, y], slopes.at[s, y], s_s.at[at], r_s.at[at], dev(e, 0, 0, 0)).start()
        hidden[s * RB : (s + 1) * RB, :] = (pre * half).astype(BF)

    def grads(s):
        turned = jnp.transpose(means[NS, :, s * RB : (s + 1) * RB, :].reshape(NY * RB, WIDE))
        for e in range(1, NY):
            src = (y + NY - e) % NY
            arrived(slopes.at[s, src], r_s.at[s * NY + e])
        slope = slopes[s].reshape(NY * RB, HID)
        g_self = jnp.dot(turned, slope, preferred_element_type=F32)
        for e in range(1, NY):
            arrived(means.at[s, (y + e) % NY], r_m.at[s * NY + e])
        turned = jnp.transpose(means[s].reshape(NY * RB, WIDE))
        return g_self, jnp.dot(turned, slope, preferred_element_type=F32)

    for d in (1, 2, 3, 0):
        plane(0, d)
    for d in range(1, NY):
        at = ((y + NY - d) % NY) * 2 + 1 - c
        arrived(wf.at[at], r_f.at[d])
    arrived(wf.at[y * 2 + 1 - c], r_f.at[0])
    for e in range(1, NY):
        arrived(theirs.at[(y + NY - e) % NY], r_o.at[e])
    activate(0)
    both = grads(0)

    for p in range(2):
        for q in range(NX):
            for w in range(2):
                at = p * COLS + q * QROW
                gsend[p * NX + q, w] = both[w][at : at + QROW].astype(BF)
    hops = [(dc, dx) for dx in range(NX) for dc in range(2) if dc or dx]
    for n, (dc, dx) in enumerate(hops):
        core = 1 - c if dc else c
        remote(gsend.at[core * NX + (x + dx) % NX], gx.at[n], s_gx.at[n], r_gx.at[n], dev(0, dc, dx, 0)).start()
    total = gsend[c * NX + x].astype(F32)
    for n in range(len(hops)):
        arrived(gx.at[n], r_gx.at[n])
        total = total + gx[n].astype(F32)
    gz[z] = total.astype(BF)
    for d in range(1, NZ):
        remote(gz.at[z], gz.at[z], s_gz.at[d], r_gz.at[d], dev(0, 0, 0, d)).start()
    for d in range(1, NZ):
        arrived(gz.at[(z + NZ - d) % NZ], r_gz.at[d])
    total = gz[0].astype(F32)
    for d in range(1, NZ):
        total = total + gz[d].astype(F32)
    gq[x] = total
    for d in range(1, NX):
        remote(gq.at[x], gq.at[x], s_gq.at[d], r_gq.at[d], dev(0, 0, d, 0)).start()
    for d in range(1, NX):
        arrived(gq.at[(x + NX - d) % NX], r_gq.at[d])
    for q in range(NX):
        gself[q * QROW : (q + 1) * QROW, :] = gq[q, 0]
        gneigh[q * QROW : (q + 1) * QROW, :] = gq[q, 1]

    left_here(feat.at[:, pl.ds(give, HALF)], s_x)
    for ref, sem in sent:
        left_here(ref, sem)
    for d in range(1, NZG):
        left_here(nbs.at[zh], s_n.at[d])
    for d in range(1, NY):
        left_here(wf.at[f_id], s_w.at[d])
        left_here(theirs.at[y], s_o.at[d])
    for d in range(NY):
        left_here(wf.at[f_id], s_f.at[d])

    def drain(at, _):
        left_here(stage.at[at], s_p.at[at])
        return 0

    for s in range(NS):
        lax.fori_loop(s * NZG * NY + 1, (s + 1) * NZG * NY, drain, 0)
        for e in range(1, NY):
            left_here(slopes.at[s, y], s_s.at[s * NY + e])
            left_here(mine.at[s * NY + e], s_m.at[s * NY + e])
    for n in range(len(hops)):
        left_here(gsend.at[0], s_gx.at[n])
    for d in range(1, NZ):
        left_here(gz.at[z], s_gz.at[d])
    for d in range(1, NX):
        left_here(gq.at[x], s_gq.at[d])


def hand_over(a, b, c, out_a, out_b, out_c):
    out_a[...] = a[...]
    out_b[...] = b[...]
    out_c[...] = c[...]


VMEM = pl.BlockSpec(memory_space=pltpu.VMEM)
SMEM = pl.BlockSpec(memory_space=pltpu.SMEM)


def sems(*counts):
    return [pltpu.SemaphoreType.DMA((n,)) if n else pltpu.SemaphoreType.DMA for n in counts for _ in range(2)]


def on_device(features, self_rows, neighbours, w_self, w_neigh, cotangent):
    shape = jax.ShapeDtypeStruct
    outs = [shape((SHARE, HID), BF), shape((COLS, HID), F32), shape((COLS, HID), F32)]
    got = pl.pallas_call(
        kernel,
        out_shape=outs,
        in_specs=[VMEM, VMEM, SMEM, VMEM, VMEM, VMEM],
        out_specs=[VMEM] * 3,
        scratch_shapes=[
            pltpu.VMEM((2, COLS, HALF), BF),
            pltpu.VMEM((GROUP, 2, HALF, WIDE), BF),
            pltpu.VMEM((TAB + 8, WIDE), F32),
            pltpu.VMEM((NZG, FAN, TGT), I32),
            pltpu.VMEM((NZG * 8, TGT), I32),
            pltpu.SMEM((NZG * 8, TGT), I32),
            pltpu.VMEM((2 * NY, 2, COLS, HID), BF),
            pltpu.VMEM((TGT, WIDE), F32),
            pltpu.VMEM((NY, SHARE, WIDE), BF),
            pltpu.VMEM((NS * NZG * NY, RB, WIDE), BF),
            pltpu.VMEM((NS * NZG * NY, RB, WIDE), BF),
            pltpu.VMEM((NS * NY, RB, WIDE), BF),
            pltpu.VMEM((NS, NY, RB, HID), BF),
            pltpu.VMEM((NS + 1, NY, SHARE, WIDE), BF),
            pltpu.VMEM((2 * NX, 2, QROW, HID), BF),
            pltpu.VMEM((2 * NX - 1, 2, QROW, HID), BF),
            pltpu.VMEM((NZ, 2, QROW, HID), BF),
            pltpu.VMEM((NX, 2, QROW, HID), F32),
            *sems(0, 30, NZG, NY, NY, NY, NS * NZG * NY, NS * NY, NS * NY, 2 * NX - 1, NZ, NX),
            pltpu.SemaphoreType.DMA,
        ],
        compiler_params=pltpu.CompilerParams(collective_id=0, has_side_effects=True, vmem_limit_bytes=56 * 2**20),
        name="layer",
    )(features.T, neighbours, self_rows, w_self, w_neigh, cotangent)
    return tuple(
        pl.pallas_call(hand_over, out_shape=outs, in_specs=[VMEM] * 3, out_specs=[VMEM] * 3, name="results")(*got)
    )


def solution(mesh):
    return jax.shard_map(
        on_device,
        mesh=mesh,
        in_specs=(
            P("node", "feat"),
            P("node"),
            P(None, "node"),
            P("feat", None),
            P("feat", None),
            P("node", None),
        ),
        out_specs=(P(("node", "feat"), None), P("feat", None), P("feat", None)),
        check_vma=False,
    )
```

```python
import math

import jax
import jax.numpy as jnp
from jax import lax
from jax.experimental import pallas as pl
from jax.experimental.pallas import tpu as pltpu
from jax.sharding import PartitionSpec as P

NX, NZ, NY = 4, 8, 8
FAN = 10
ROWS = 2048
HALF = ROWS // 2
UNIT = HALF // 2
COLS = 64
WIDE = 2 * COLS
HID = 256
SHARE = 64
TGT = NY * SHARE
GROUP = 2 * NX
NZG = NZ // 2
TAB = GROUP * ROWS
QROW = COLS // NX
NS = 1
RB = SHARE // NS
AT_ONCE = 8
LISTS = NZG * FAN * TGT
MESH = pl.DeviceIdType.MESH
ROOT = math.sqrt(2.0 / math.pi)
BF, F32, I32 = jnp.bfloat16, jnp.float32, jnp.int32


def kernel(
    feat, nb, rows, ws, wn, cot, hidden, gself, gneigh,
    pieces, tab, wide, nbs, lists, idx, wf, own, theirs, stage, pin, mine, slopes, means, mates,
    gsend, gx, gz, gq,
    s_x, r_x, s_t, r_t, s_n, r_n, s_w, r_w, s_f, r_f, s_o, r_o, s_p, r_p, s_s, r_s, s_m, r_m,
    s_gx, r_gx, s_gz, r_gz, s_gq, r_gq, s_idx,
):
    f_id, n_id = lax.axis_index("feat"), lax.axis_index("node")
    y, c, x, z = f_id // 2, f_id % 2, n_id // NZ, n_id % NZ
    zl, zh = z % 2, z // 2

    def dev(dy, dc, dx, dz):
        core = 1 - c if dc else c
        return {"feat": ((y + dy) % NY) * 2 + core, "node": ((x + dx) % NX) * NZ + (z + dz) % NZ}

    partner = dev(0, 1, 0, 0)
    right, left = dev(0, 0, 1, 0), dev(0, 0, NX - 1, 0)
    over = {"feat": f_id, "node": x * NZ + z + 1 - 2 * zl}

    def remote(src, dst, send, recv, to):
        return pltpu.make_async_remote_copy(
            src_ref=src, dst_ref=dst, send_sem=send, recv_sem=recv, device_id=to, device_id_type=MESH
        )

    def arrived(ref, recv):
        remote(ref, ref, recv, recv, partner).wait_recv()

    def left_here(ref, send):
        remote(ref, ref, send, send, partner).wait_send()

    barrier = pltpu.get_barrier_semaphore()
    friends = [partner]
    friends += [dev(0, 0, 0, d) for d in range(1, NZ)]
    friends += [dev(0, dc, d, 0) for d in range(1, NX) for dc in range(2)]
    friends += [dev(e, 0, 0, 2 * d) for d in range(NZG) for e in range(1, NY)]
    for to in friends:
        pl.semaphore_signal(barrier, inc=1, device_id=to, device_id_type=MESH)

    wf[f_id, 0] = ws[...]
    wf[f_id, 1] = wn[...]
    cuts = []
    for b in range(NY):
        lo = nb[:, b * 128 : b * 128 + 64]
        hi = nb[:, b * 128 + 64 : b * 128 + 128]
        cuts.append(jnp.where(c == 0, lo, hi))
    nbs[zh] = jnp.concatenate(cuts, axis=1)
    give = pl.multiple_of((1 - c) * HALF, HALF)
    keep = pl.multiple_of(c * HALF, HALF)
    pieces[c] = feat[:, pl.ds(keep, HALF)]

    pl.semaphore_wait(barrier, len(friends))

    swap = remote(feat.at[:, pl.ds(give, HALF)], pieces.at[c], s_x, r_x, partner)
    swap.start()
    for d in range(1, NZG):
        remote(nbs.at[zh], nbs.at[zh], s_n.at[d], r_n.at[d], dev(0, 0, 0, 2 * d)).start()
    arrived(pieces.at[1 - c], r_x)
    home = x * 2 + zl

    def turn(i, _):
        at = pl.multiple_of(i * 256, 256)
        block = pieces[:, :, pl.ds(at, 256)].reshape(WIDE, 256)
        tab[home, c, pl.ds(at, 256), :] = jnp.transpose(block)
        return 0

    lax.fori_loop(0, HALF // 256, turn, 0)

    xr, xl, far, zo = (x + 1) % NX, (x + NX - 1) % NX, (x + 2) % NX, 1 - zl

    def unit(i, zz, h, core):
        return tab.at[i * 2 + zz, core, pl.ds(h * UNIT, UNIT)]

    def widen(i, zz, h, core):
        base = ((i * 2 + zz) * 2 + core) * HALF + h * UNIT

        def step(k, _):
            at = pl.multiple_of(k * 128, 128)
            piece = tab[i * 2 + zz, core, pl.ds(h * UNIT + at, 128), :]
            wide[pl.ds(pl.multiple_of(base + at, 128), 128), :] = piece.astype(F32)
            return 0

        lax.fori_loop(0, UNIT // 128, step, 0)

    sent = []

    def go(m, i, zz, h, to):
        ref = unit(i, zz, h, c)
        remote(ref, ref, s_t.at[m], r_t.at[m], to).start()
        sent.append((ref, s_t.at[m]))

    passed = []

    def pass_on(i, zz, h):
        m = 14 + len(passed)
        go(m, i, zz, h, partner)
        passed.append((m, i, zz, h))

    def come(m, i, zz, h):
        arrived(unit(i, zz, h, c), r_t.at[m])

    def fetch_own(k, _):
        first = (k // 8) * 128 + c * SHARE + (k % 8) * 8
        for u in range(8):
            own[pl.ds(k * 8 + u, 1), :] = wide[pl.ds(home * ROWS + rows[first + u], 1), :]
        return 0

    go(0, x, zl, 0, right)
    go(3, x, zl, 1, left)
    go(4, x, zl, 0, over)
    go(5, x, zl, 1, over)
    pass_on(x, zl, 0)
    pass_on(x, zl, 1)
    widen(x, zl, 0, c)
    widen(x, zl, 1, c)
    arrived(unit(x, zl, 0, 1 - c), r_t.at[14])
    widen(x, zl, 0, 1 - c)
    arrived(unit(x, zl, 1, 1 - c), r_t.at[15])
    widen(x, zl, 1, 1 - c)
    go(1, x, zl, 1, right)
    go(2, x, zl, 0, left)

    lax.fori_loop(0, TGT // 8, fetch_own, 0)
    mates[...] = own[...].astype(BF).reshape(NY, SHARE, WIDE)
    theirs[y] = mates[y]
    for e in range(1, NY):
        remote(mates.at[(y + e) % NY], theirs.at[y], s_o.at[e], r_o.at[e], dev(e, 0, 0, 0)).start()
    come(0, xl, zl, 0)
    go(6, xl, zl, 0, right)
    come(3, xr, zl, 1)
    go(7, xr, zl, 1, left)
    pass_on(xl, zl, 0)
    pass_on(xr, zl, 1)
    for d in range(1, NZG):
        at = (zh + NZG - d) % NZG
        arrived(nbs.at[at], r_n.at[d])
    for g in range(NZG):
        n = nbs[g]
        part_of = n >> 11
        inside = ((part_of & 7) >> 1) == zh
        row = ((((part_of >> 3) << 1) | (part_of & 1)) << 11) | (n & (ROWS - 1))
        lists[g] = jnp.where(inside, row, TAB)
    to_scalar = [
        pltpu.make_async_copy(lists.at[g, f], idx.at[pl.ds((g * FAN + f) * TGT, TGT)], s_idx.at[g * FAN + f])
        for g in range(NZG)
        for f in range(FAN)
    ]
    for copy in to_scalar:
        copy.start()

    for d in range(1, NY):
        remote(wf.at[f_id], wf.at[f_id], s_w.at[d], r_w.at[d], dev(d, 0, 0, 0)).start()
    remote(wf.at[f_id], wf.at[f_id], s_f.at[0], r_f.at[0], partner).start()
    come(4, x, zo, 0)
    pass_on(x, zo, 0)
    come(5, x, zo, 1)
    pass_on(x, zo, 1)
    widen(xl, zl, 0, c)
    widen(xr, zl, 1, c)
    widen(x, zo, 0, c)
    come(1, xl, zl, 1)
    pass_on(xl, zl, 1)
    come(2, xr, zl, 0)
    pass_on(xr, zl, 0)
    come(6, far, zl, 0)
    go(12, far, zl, 0, over)
    come(7, far, zl, 1)
    go(13, far, zl, 1, over)
    go(8, x, zo, 0, right)
    go(11, x, zo, 1, left)
    go(10, x, zo, 1, right)
    go(9, x, zo, 0, left)
    pass_on(far, zl, 0)
    pass_on(far, zl, 1)
    widen(x, zo, 1, c)
    widen(xl, zl, 1, c)
    widen(xr, zl, 0, c)
    widen(far, zl, 0, c)
    widen(far, zl, 1, c)
    order = ((8, xl, 0), (11, xr, 1), (10, xl, 1), (9, xr, 0))
    for m, i, h in order:
        come(m, i, zo, h)
        pass_on(i, zo, h)
    come(12, far, zo, 0)
    pass_on(far, zo, 0)
    for m, i, h in order:
        widen(i, zo, h, c)
    come(13, far, zo, 1)
    pass_on(far, zo, 1)
    widen(far, zo, 0, c)
    widen(far, zo, 1, c)
    for m, i, zz, h in passed[2:]:
        arrived(unit(i, zz, h, 1 - c), r_t.at[m])
        widen(i, zz, h, 1 - c)
    wide[pl.ds(TAB, 8), :] = jnp.zeros((8, WIDE), F32)
    for copy in to_scalar:
        copy.wait()

    def total_of(g, b, s):
        start = g * (FAN * TGT) + b * SHARE + s * RB

        def some(k, _):
            first = start + k * AT_ONCE
            for u in range(AT_ONCE):
                total = None
                for f in range(FAN):
                    skip = f * TGT + u
                    row = wide[pl.ds(idx.at[pl.ds(skip, LISTS - skip)][first], 1), :]
                    total = row if total is None else total + row
                own[pl.ds(k * AT_ONCE + u, 1), :] = total
            return 0

        lax.fori_loop(0, RB // AT_ONCE, some, 0)

    def plane(s, d):
        g = (zh + d) % NZG

        def one(e, _):
            at = (s * NZG + d) * NY + e
            total_of(g, (y + e) % NY, s)
            stage[at] = own[pl.ds(0, RB), :].astype(BF)
            remote(stage.at[at], pin.at[at], s_p.at[at], r_p.at[at], dev(0, 0, 0, 2 * d)).start()
            return 0

        lax.fori_loop(0, NY, one, 0)

    def finish(s, e):
        b = (y + e) % NY
        total_of(zh, b, s)
        total = own[pl.ds(0, RB), :]
        for d in range(1, NZG):
            at = (s * NZG + d) * NY + e
            arrived(pin.at[at], r_p.at[at])
            total = total + pin[at].astype(F32)
        means[s, b] = (total * (1.0 / FAN)).astype(BF)

    def home_plane(s):
        def one(e, _):
            at = s * NY + e
            finish(s, e)
            remote(means.at[s, (y + e) % NY], mine.at[s, y], s_m.at[at], r_m.at[at], dev(e, 0, 0, 0)).start()
            return 0

        lax.fori_loop(1, NY, one, 0)
        finish(s, 0)
        mine[s, y] = means[s, y]

    def activate(s):
        pre = jnp.zeros((RB, HID), F32)
        for e in range(NY):
            src = (y + NY - e) % NY
            w_own = jnp.concatenate([wf[2 * src, 0], wf[2 * src + 1, 0]], axis=0)
            w_mean = jnp.concatenate([wf[2 * src, 1], wf[2 * src + 1, 1]], axis=0)
            pre = pre + jnp.dot(theirs[src, s * RB : (s + 1) * RB, :], w_own, preferred_element_type=F32)
            if e:
                arrived(mine.at[s, src], r_m.at[s * NY + e])
            pre = pre + jnp.dot(mine[s, src], w_mean, preferred_element_type=F32)
        square = pre * pre
        th = jnp.tanh(ROOT * (pre + 0.044715 * (square * pre)))
        half = 0.5 * (1.0 + th)
        dydx = half + 0.5 * pre * (1.0 - th * th) * (ROOT * (1.0 + 3.0 * 0.044715 * square))
        first = pl.multiple_of(f_id * SHARE + s * RB, RB)
        slopes[s, y] = (cot[pl.ds(first, RB), :].astype(F32) * dydx).astype(BF)
        for e in range(1, NY):
            at = s * NY + e
            remote(slopes.at[s, y], slopes.at[s, y], s_s.at[at], r_s.at[at], dev(e, 0, 0, 0)).start()
        hidden[s * RB : (s + 1) * RB, :] = (pre * half).astype(BF)

    def grads(s):
        mates_turned = jnp.transpose(mates[:, s * RB : (s + 1) * RB, :].reshape(NY * RB, WIDE))
        means_turned = jnp.transpose(means[s].reshape(NY * RB, WIDE))
        for e in range(1, NY):
            src = (y + NY - e) % NY
            arrived(slopes.at[s, src], r_s.at[s * NY + e])
        slope = slopes[s].reshape(NY * RB, HID)
        return [jnp.dot(t, slope, preferred_element_type=F32) for t in (mates_turned, means_turned)]

    plane(0, 2)
    plane(0, 1)
    for d in range(1, NY):
        at = ((y + NY - d) % NY) * 2 + c
        arrived(wf.at[at], r_w.at[d])
        remote(wf.at[at], wf.at[at], s_f.at[d], r_f.at[d], partner).start()
    plane(0, 3)
    home_plane(0)
    for d in range(1, NY):
        at = ((y + NY - d) % NY) * 2 + 1 - c
        arrived(wf.at[at], r_f.at[d])
    arrived(wf.at[y * 2 + 1 - c], r_f.at[0])
    for e in range(1, NY):
        arrived(theirs.at[(y + NY - e) % NY], r_o.at[e])
    activate(0)
    both = grads(0)

    for p in range(2):
        for q in range(NX):
            for w in range(2):
                at = p * COLS + q * QROW
                gsend[p * NX + q, w] = both[w][at : at + QROW].astype(BF)
    hops = [(dc, dx) for dx in range(NX) for dc in range(2) if dc or dx]
    for n, (dc, dx) in enumerate(hops):
        core = 1 - c if dc else c
        remote(gsend.at[core * NX + (x + dx) % NX], gx.at[n], s_gx.at[n], r_gx.at[n], dev(0, dc, dx, 0)).start()
    total = gsend[c * NX + x].astype(F32)
    for n in range(len(hops)):
        arrived(gx.at[n], r_gx.at[n])
        total = total + gx[n].astype(F32)
    gz[z] = total.astype(BF)
    for d in range(1, NZ):
        remote(gz.at[z], gz.at[z], s_gz.at[d], r_gz.at[d], dev(0, 0, 0, d)).start()
    for d in range(1, NZ):
        arrived(gz.at[(z + NZ - d) % NZ], r_gz.at[d])
    total = gz[0].astype(F32)
    for d in range(1, NZ):
        total = total + gz[d].astype(F32)
    gq[x] = total
    for d in range(1, NX):
        remote(gq.at[x], gq.at[x], s_gq.at[d], r_gq.at[d], dev(0, 0, d, 0)).start()
    for d in range(1, NX):
        arrived(gq.at[(x + NX - d) % NX], r_gq.at[d])
    for q in range(NX):
        gself[q * QROW : (q + 1) * QROW, :] = gq[q, 0]
        gneigh[q * QROW : (q + 1) * QROW, :] = gq[q, 1]

    left_here(feat.at[:, pl.ds(give, HALF)], s_x)
    for ref, sem in sent:
        left_here(ref, sem)
    for d in range(1, NZG):
        left_here(nbs.at[zh], s_n.at[d])
    for d in range(1, NY):
        left_here(wf.at[f_id], s_w.at[d])
        left_here(theirs.at[y], s_o.at[d])
    for d in range(NY):
        left_here(wf.at[f_id], s_f.at[d])

    def drain(at, _):
        left_here(stage.at[at], s_p.at[at])
        return 0

    for s in range(NS):
        lax.fori_loop((s * NZG + 1) * NY, (s + 1) * NZG * NY, drain, 0)
        for e in range(1, NY):
            left_here(slopes.at[s, y], s_s.at[s * NY + e])
            left_here(mine.at[s, y], s_m.at[s * NY + e])
    for n in range(len(hops)):
        left_here(gsend.at[0], s_gx.at[n])
    for d in range(1, NZ):
        left_here(gz.at[z], s_gz.at[d])
    for d in range(1, NX):
        left_here(gq.at[x], s_gq.at[d])


def hand_over(a, b, c, out_a, out_b, out_c):
    out_a[...] = a[...]
    out_b[...] = b[...]
    out_c[...] = c[...]


VMEM = pl.BlockSpec(memory_space=pltpu.VMEM)
SMEM = pl.BlockSpec(memory_space=pltpu.SMEM)


def sems(*counts):
    return [pltpu.SemaphoreType.DMA((n,)) if n else pltpu.SemaphoreType.DMA for n in counts for _ in range(2)]


def on_device(features, self_rows, neighbours, w_self, w_neigh, cotangent):
    shape = jax.ShapeDtypeStruct
    outs = [shape((SHARE, HID), BF), shape((COLS, HID), F32), shape((COLS, HID), F32)]
    got = pl.pallas_call(
        kernel,
        out_shape=outs,
        in_specs=[VMEM, VMEM, SMEM, VMEM, VMEM, VMEM],
        out_specs=[VMEM] * 3,
        scratch_shapes=[
            pltpu.VMEM((2, COLS, HALF), BF),
            pltpu.VMEM((GROUP, 2, HALF, WIDE), BF),
            pltpu.VMEM((TAB + 8, WIDE), F32),
            pltpu.VMEM((NZG, FAN, TGT), I32),
            pltpu.VMEM((NZG, FAN, TGT), I32),
            pltpu.SMEM((LISTS,), I32),
            pltpu.VMEM((2 * NY, 2, COLS, HID), BF),
            pltpu.VMEM((TGT, WIDE), F32),
            pltpu.VMEM((NY, SHARE, WIDE), BF),
            pltpu.VMEM((NS * NZG * NY, RB, WIDE), BF),
            pltpu.VMEM((NS * NZG * NY, RB, WIDE), BF),
            pltpu.VMEM((NS, NY, RB, WIDE), BF),
            pltpu.VMEM((NS, NY, RB, HID), BF),
            pltpu.VMEM((NS, NY, RB, WIDE), BF),
            pltpu.VMEM((NY, SHARE, WIDE), BF),
            pltpu.VMEM((2 * NX, 2, QROW, HID), BF),
            pltpu.VMEM((2 * NX - 1, 2, QROW, HID), BF),
            pltpu.VMEM((NZ, 2, QROW, HID), BF),
            pltpu.VMEM((NX, 2, QROW, HID), F32),
            *sems(0, 30, NZG, NY, NY, NY, NS * NZG * NY, NS * NY, NS * NY, 2 * NX - 1, NZ, NX),
            pltpu.SemaphoreType.DMA((NZG * FAN,)),
        ],
        compiler_params=pltpu.CompilerParams(collective_id=0, has_side_effects=True, vmem_limit_bytes=56 * 2**20),
        name="layer",
    )(features.T, neighbours, self_rows, w_self, w_neigh, cotangent)
    return tuple(
        pl.pallas_call(hand_over, out_shape=outs, in_specs=[VMEM] * 3, out_specs=[VMEM] * 3, name="results")(*got)
    )


def solution(mesh):
    return jax.shard_map(
        on_device,
        mesh=mesh,
        in_specs=(
            P("node", "feat"),
            P("node"),
            P(None, "node"),
            P("feat", None),
            P("feat", None),
            P("node", None),
        ),
        out_specs=(P(("node", "feat"), None), P("feat", None), P("feat", None)),
        check_vma=False,
    )
```

```python
import math

import jax
import jax.numpy as jnp
from jax import lax
from jax.experimental import pallas as pl
from jax.experimental.pallas import tpu as pltpu
from jax.sharding import PartitionSpec as P

NX, NZ, NY = 4, 8, 8
FAN = 10
PAIR = FAN // 2
ROWS = 2048
HALF = ROWS // 2
UNIT = HALF // 2
COLS = 64
WIDE = 2 * COLS
HID = 256
SHARE = 64
TGT = NY * SHARE
GROUP = 2 * NX
NZG = NZ // 2
TAB = GROUP * ROWS
QROW = COLS // NX
NS = 1
RB = SHARE // NS
AT_ONCE = 8
LISTS = NZG * FAN * TGT
MESH = pl.DeviceIdType.MESH
ROOT = math.sqrt(2.0 / math.pi)
BF, F32, I32 = jnp.bfloat16, jnp.float32, jnp.int32


def kernel(
    feat, nb, rows, ws, wn, cot, hidden, gself, gneigh,
    all_nb, my_cot, pieces, tab, wide, nbs, lists, idx, wf, own, theirs, stage, pin, mine, slopes, means, mates,
    gsend, gx, gz, gq,
    s_x, r_x, s_t, r_t, s_h, r_h, s_n, r_n, s_w, r_w, s_f, r_f, s_o, r_o, s_p, r_p, s_s, r_s, s_m, r_m,
    s_gx, r_gx, s_gz, r_gz, s_gq, r_gq, s_idx, s_in,
):
    f_id, n_id = lax.axis_index("feat"), lax.axis_index("node")
    y, c, x, z = f_id // 2, f_id % 2, n_id // NZ, n_id % NZ
    zl, zh = z % 2, z // 2

    def dev(dy, dc, dx, dz):
        core = 1 - c if dc else c
        return {"feat": ((y + dy) % NY) * 2 + core, "node": ((x + dx) % NX) * NZ + (z + dz) % NZ}

    partner = dev(0, 1, 0, 0)
    right, left = dev(0, 0, 1, 0), dev(0, 0, NX - 1, 0)
    over = {"feat": f_id, "node": x * NZ + z + 1 - 2 * zl}

    def remote(src, dst, send, recv, to):
        return pltpu.make_async_remote_copy(
            src_ref=src, dst_ref=dst, send_sem=send, recv_sem=recv, device_id=to, device_id_type=MESH
        )

    def arrived(ref, recv):
        remote(ref, ref, recv, recv, partner).wait_recv()

    def left_here(ref, send):
        remote(ref, ref, send, send, partner).wait_send()

    barrier = pltpu.get_barrier_semaphore()
    friends = [partner]
    friends += [dev(0, 0, 0, d) for d in range(1, NZ)]
    friends += [dev(0, dc, d, 0) for d in range(1, NX) for dc in range(2)]
    friends += [dev(e, 0, 0, 2 * d) for d in range(NZG) for e in range(1, NY)]
    for to in friends:
        pl.semaphore_signal(barrier, inc=1, device_id=to, device_id_type=MESH)

    give = pl.multiple_of((1 - c) * HALF, HALF)
    keep = pl.multiple_of(c * HALF, HALF)
    loads = [
        pltpu.make_async_copy(src, dst, s_in.at[n])
        for n, (src, dst) in enumerate(
            (
                (feat.at[:, pl.ds(keep, HALF)], pieces.at[c]),
                (nb, all_nb),
                (ws, wf.at[f_id, 0]),
                (wn, wf.at[f_id, 1]),
                (cot.at[pl.ds(pl.multiple_of(f_id * SHARE, SHARE), SHARE)], my_cot),
            )
        )
    ]
    for load in loads:
        load.start()

    pl.semaphore_wait(barrier, len(friends))

    swap = remote(feat.at[:, pl.ds(give, HALF)], pieces.at[c], s_x, r_x, partner)
    swap.start()
    loads[0].wait()
    arrived(pieces.at[1 - c], r_x)
    home = x * 2 + zl

    def turn(i, _):
        at = pl.multiple_of(i * 256, 256)
        block = pieces[:, :, pl.ds(at, 256)].reshape(WIDE, 256)
        tab[home, c, pl.ds(at, 256), :] = jnp.transpose(block)
        return 0

    lax.fori_loop(0, HALF // 256, turn, 0)

    xr, xl, far, zo = (x + 1) % NX, (x + NX - 1) % NX, (x + 2) % NX, 1 - zl

    def unit(i, zz, h, core):
        return tab.at[i * 2 + zz, core, pl.ds(h * UNIT, UNIT)]

    def widen(i, zz, h, core):
        base = ((i * 2 + zz) * 2 + core) * HALF + h * UNIT

        def step(k, _):
            at = pl.multiple_of(k * 128, 128)
            piece = tab[i * 2 + zz, core, pl.ds(h * UNIT + at, 128), :]
            wide[pl.ds(pl.multiple_of(base + at, 128), 128), :] = piece.astype(F32)
            return 0

        lax.fori_loop(0, UNIT // 128, step, 0)

    def go(m, i, zz, h, to):
        ref = unit(i, zz, h, c)
        remote(ref, ref, s_t.at[m // 2], r_t.at[m], to).start()

    def passing(i, zz):
        return s_h.at[i * 2 + zz], r_h.at[i * 2 + zz]

    def pass_on(i, zz, h):
        ref = unit(i, zz, h, c)
        send, recv = passing(i, zz)
        remote(ref, ref, send, recv, partner).start()

    def taken(i, zz):
        arrived(tab.at[i * 2 + zz, 1 - c], passing(i, zz)[1])
        for h in range(2):
            widen(i, zz, h, 1 - c)

    def come(m, i, zz, h):
        arrived(unit(i, zz, h, c), r_t.at[m])

    def fetch_own(k, _):
        first = (k // 8) * 128 + c * SHARE + (k % 8) * 8
        for u in range(8):
            own[pl.ds(k * 8 + u, 1), :] = wide[pl.ds(home * ROWS + rows[first + u], 1), :]
        return 0

    go(0, x, zl, 0, right)
    go(3, x, zl, 1, left)
    go(4, x, zl, 0, over)
    pass_on(x, zl, 0)
    pass_on(x, zl, 1)

    loads[1].wait()
    cuts = []
    for b in range(NY):
        lo = all_nb[:, b * 128 : b * 128 + 64]
        hi = all_nb[:, b * 128 + 64 : b * 128 + 128]
        cuts.append(jnp.where(c == 0, lo, hi))
    named = jnp.concatenate(cuts, axis=1)
    nbs[zh] = named[:PAIR] | (named[PAIR:] << 16)
    widen(x, zl, 0, c)
    widen(x, zl, 1, c)
    taken(x, zl)
    go(1, x, zl, 1, right)
    go(2, x, zl, 0, left)
    go(5, x, zl, 1, over)
    loads[2].wait()
    loads[3].wait()
    loads[4].wait()
    for d in range(1, NY):
        remote(wf.at[f_id], wf.at[f_id], s_w, r_w, dev(d, 0, 0, 0)).start()
    remote(wf.at[f_id], wf.at[f_id], s_f, r_f, partner).start()

    lax.fori_loop(0, TGT // 8, fetch_own, 0)
    mates[...] = own[...].astype(BF).reshape(NY, SHARE, WIDE)
    theirs[y] = mates[y]
    for e in range(1, NY):
        remote(mates.at[(y + e) % NY], theirs.at[y], s_o, r_o, dev(e, 0, 0, 0)).start()

    come(0, xl, zl, 0)
    go(6, xl, zl, 0, right)
    go(11, xl, zl, 0, over)
    come(3, xr, zl, 1)
    go(7, xr, zl, 1, left)
    go(12, xr, zl, 1, over)
    come(4, x, zo, 0)
    go(8, x, zo, 0, dev(0, 0, 2, 0))
    go(10, x, zo, 0, left)
    pass_on(xl, zl, 0)
    pass_on(xr, zl, 1)
    pass_on(x, zo, 0)
    for d in range(1, NZG):
        remote(nbs.at[zh], nbs.at[zh], s_n.at[d], r_n.at[d], dev(0, 0, 0, 2 * d)).start()
    widen(xl, zl, 0, c)
    widen(xr, zl, 1, c)
    come(1, xl, zl, 1)
    go(13, xl, zl, 1, over)
    come(5, x, zo, 1)
    go(9, x, zo, 1, dev(0, 0, 2, 0))
    come(2, xr, zl, 0)
    pass_on(xl, zl, 1)
    pass_on(xr, zl, 0)
    pass_on(x, zo, 1)
    widen(x, zo, 0, c)
    widen(xl, zl, 1, c)
    widen(xr, zl, 0, c)
    widen(x, zo, 1, c)
    come(6, far, zl, 0)
    pass_on(far, zl, 0)
    come(7, far, zl, 1)
    pass_on(far, zl, 1)
    widen(far, zl, 0, c)
    widen(far, zl, 1, c)

    for d in range(1, NZG):
        at = (zh + NZG - d) % NZG
        arrived(nbs.at[at], r_n.at[d])
    for g in range(NZG):
        words = nbs[g]
        for h, n in enumerate((words & 0xFFFF, (words >> 16) & 0xFFFF)):
            part_of = n >> 11
            inside = ((part_of & 7) >> 1) == zh
            row = ((((part_of >> 3) << 1) | (part_of & 1)) << 11) | (n & (ROWS - 1))
            lists[g, h * PAIR : (h + 1) * PAIR, :] = jnp.where(inside, row, TAB)
    to_scalar = [
        pltpu.make_async_copy(lists.at[g, f], idx.at[pl.ds((g * FAN + f) * TGT, TGT)], s_idx)
        for g in range(NZG)
        for f in range(FAN)
    ]
    for copy in to_scalar:
        copy.start()
    rest = ((11, xl, 0), (12, xr, 1), (10, xr, 0), (8, far, 0), (13, xl, 1), (9, far, 1))
    for m, i, h in rest:
        come(m, i, zo, h)
        pass_on(i, zo, h)
    for m, i, h in rest:
        widen(i, zo, h, c)
    for i, zz in ((xl, zl), (xr, zl), (x, zo), (far, zl), (xr, zo), (xl, zo), (far, zo)):
        taken(i, zz)
    wide[pl.ds(TAB, 8), :] = jnp.zeros((8, WIDE), F32)
    pltpu.make_async_copy(idx, idx, s_idx).wait()

    def total_of(g, b, s):
        start = g * (FAN * TGT) + b * SHARE + s * RB

        def some(k, _):
            first = start + k * AT_ONCE
            for u in range(AT_ONCE):
                total = None
                for f in range(FAN):
                    skip = f * TGT + u
                    row = wide[pl.ds(idx.at[pl.ds(skip, LISTS - skip)][first], 1), :]
                    total = row if total is None else total + row
                own[pl.ds(k * AT_ONCE + u, 1), :] = total
            return 0

        lax.fori_loop(0, RB // AT_ONCE, some, 0)

    def plane(s, d):
        g = (zh + d) % NZG

        def one(e, _):
            total_of(g, (y + e) % NY, s)
            stage[e, d - 1] = own[pl.ds(0, RB), :].astype(BF)
            remote(stage.at[e, d - 1], pin.at[e, d - 1], s_p, r_p.at[e], dev(0, 0, 0, 2 * d)).start()
            return 0

        lax.fori_loop(0, NY, one, 0)

    def finish(s, e):
        b = (y + e) % NY
        total_of(zh, b, s)
        total = own[pl.ds(0, RB), :]
        arrived(pin.at[e], r_p.at[e])
        for d in range(NZG - 1):
            total = total + pin[e, d].astype(F32)
        means[s, b] = (total * (1.0 / FAN)).astype(BF)

    def home_plane(s):
        def one(e, _):
            finish(s, e)
            remote(means.at[s, (y + e) % NY], mine.at[s, y], s_m, r_m, dev(e, 0, 0, 0)).start()
            return 0

        lax.fori_loop(1, NY, one, 0)
        finish(s, 0)
        mine[s, y] = means[s, y]

    def activate(s):
        pre = jnp.zeros((RB, HID), F32)
        for b in range(NY):
            w_own = jnp.concatenate([wf[2 * b, 0], wf[2 * b + 1, 0]], axis=0)
            pre = pre + jnp.dot(theirs[b, s * RB : (s + 1) * RB, :], w_own, preferred_element_type=F32)
        for e in range(NY):
            src = (y + NY - e) % NY
            w_mean = jnp.concatenate([wf[2 * src, 1], wf[2 * src + 1, 1]], axis=0)
            if e == 0:
                arrived(mine.at[s, pl.ds(0, NY - 1)], r_m)
            pre = pre + jnp.dot(mine[s, src], w_mean, preferred_element_type=F32)
        square = pre * pre
        th = jnp.tanh(ROOT * (pre + 0.044715 * (square * pre)))
        half = 0.5 * (1.0 + th)
        dydx = half + 0.5 * pre * (1.0 - th * th) * (ROOT * (1.0 + 3.0 * 0.044715 * square))
        slopes[s, y] = (my_cot[s * RB : (s + 1) * RB, :].astype(F32) * dydx).astype(BF)
        for e in range(1, NY):
            remote(slopes.at[s, y], slopes.at[s, y], s_s, r_s, dev(e, 0, 0, 0)).start()
        hidden[s * RB : (s + 1) * RB, :] = (pre * half).astype(BF)

    def grads(s):
        mates_turned = jnp.transpose(mates[:, s * RB : (s + 1) * RB, :].reshape(NY * RB, WIDE))
        means_turned = jnp.transpose(means[s].reshape(NY * RB, WIDE))
        arrived(slopes.at[s, pl.ds(0, NY - 1)], r_s)
        slope = slopes[s].reshape(NY * RB, HID)
        return [jnp.dot(t, slope, preferred_element_type=F32) for t in (mates_turned, means_turned)]

    plane(0, 2)
    plane(0, 1)
    arrived(wf.at[pl.ds(0, NY - 1)], r_w)
    for d in range(1, NY):
        at = ((y + NY - d) % NY) * 2 + c
        remote(wf.at[at], wf.at[at], s_f, r_f, partner).start()
    plane(0, 3)
    home_plane(0)
    arrived(wf.at[pl.ds(0, NY)], r_f)
    arrived(theirs.at[pl.ds(0, NY - 1)], r_o)
    activate(0)
    both = grads(0)

    for p in range(2):
        for q in range(NX):
            for w in range(2):
                at = p * COLS + q * QROW
                gsend[p * NX + q, w] = both[w][at : at + QROW].astype(BF)
    hops = [(dc, dx) for dx in range(NX) for dc in range(2) if dc or dx]
    for n, (dc, dx) in enumerate(hops):
        core = 1 - c if dc else c
        remote(gsend.at[core * NX + (x + dx) % NX], gx.at[n], s_gx, r_gx, dev(0, dc, dx, 0)).start()
    total = gsend[c * NX + x].astype(F32)
    arrived(gx, r_gx)
    for n in range(len(hops)):
        total = total + gx[n].astype(F32)
    gz[z] = total.astype(BF)
    for d in range(1, NZ):
        remote(gz.at[z], gz.at[z], s_gz, r_gz, dev(0, 0, 0, d)).start()
    arrived(gz.at[pl.ds(0, NZ - 1)], r_gz)
    total = gz[0].astype(F32)
    for d in range(1, NZ):
        total = total + gz[d].astype(F32)
    gq[x] = total
    for d in range(1, NX):
        remote(gq.at[x], gq.at[x], s_gq, r_gq, dev(0, 0, d, 0)).start()
    arrived(gq.at[pl.ds(0, NX - 1)], r_gq)
    for q in range(NX):
        gself[q * QROW : (q + 1) * QROW, :] = gq[q, 0]
        gneigh[q * QROW : (q + 1) * QROW, :] = gq[q, 1]

    left_here(feat.at[:, pl.ds(give, HALF)], s_x)
    for m in range(7):
        left_here(tab.at[home, c], s_t.at[m])
    for m in range(GROUP):
        left_here(tab.at[home, c], s_h.at[m])
    for d in range(1, NZG):
        left_here(nbs.at[zh], s_n.at[d])
    left_here(wf.at[pl.ds(0, NY - 1)], s_w)
    left_here(theirs.at[pl.ds(0, NY - 1)], s_o)
    left_here(wf.at[pl.ds(0, NY)], s_f)

    left_here(stage, s_p)
    left_here(mine.at[0, pl.ds(0, NY - 1)], s_m)
    left_here(slopes.at[0, pl.ds(0, NY - 1)], s_s)
    left_here(gx, s_gx)
    left_here(gz.at[pl.ds(0, NZ - 1)], s_gz)
    left_here(gq.at[pl.ds(0, NX - 1)], s_gq)


def hand_over(a, b, c, out_a, out_b, out_c):
    out_a[...] = a[...]
    out_b[...] = b[...]
    out_c[...] = c[...]


VMEM = pl.BlockSpec(memory_space=pltpu.VMEM)
SMEM = pl.BlockSpec(memory_space=pltpu.SMEM)
HBM = pl.BlockSpec(memory_space=pl.ANY)


def sems(*counts):
    return [pltpu.SemaphoreType.DMA((n,)) if n else pltpu.SemaphoreType.DMA for n in counts for _ in range(2)]


def on_device(features, self_rows, neighbours, w_self, w_neigh, cotangent):
    shape = jax.ShapeDtypeStruct
    outs = [shape((SHARE, HID), BF), shape((COLS, HID), F32), shape((COLS, HID), F32)]
    got = pl.pallas_call(
        kernel,
        out_shape=outs,
        in_specs=[HBM, HBM, SMEM, HBM, HBM, HBM],
        out_specs=[VMEM] * 3,
        scratch_shapes=[
            pltpu.VMEM((FAN, 2 * TGT), I32),
            pltpu.VMEM((SHARE, HID), BF),
            pltpu.VMEM((2, COLS, HALF), BF),
            pltpu.VMEM((GROUP, 2, HALF, WIDE), BF),
            pltpu.VMEM((TAB + 8, WIDE), F32),
            pltpu.VMEM((NZG, PAIR, TGT), I32),
            pltpu.VMEM((NZG, FAN, TGT), I32),
            pltpu.SMEM((LISTS,), I32),
            pltpu.VMEM((2 * NY, 2, COLS, HID), BF),
            pltpu.VMEM((TGT, WIDE), F32),
            pltpu.VMEM((NY, SHARE, WIDE), BF),
            pltpu.VMEM((NY, NZG - 1, RB, WIDE), BF),
            pltpu.VMEM((NY, NZG - 1, RB, WIDE), BF),
            pltpu.VMEM((NS, NY, RB, WIDE), BF),
            pltpu.VMEM((NS, NY, RB, HID), BF),
            pltpu.VMEM((NS, NY, RB, WIDE), BF),
            pltpu.VMEM((NY, SHARE, WIDE), BF),
            pltpu.VMEM((2 * NX, 2, QROW, HID), BF),
            pltpu.VMEM((2 * NX - 1, 2, QROW, HID), BF),
            pltpu.VMEM((NZ, 2, QROW, HID), BF),
            pltpu.VMEM((NX, 2, QROW, HID), F32),
            *sems(0),
            *(pltpu.SemaphoreType.DMA((n,)) for n in (7, 14, GROUP, GROUP, NZG, NZG)),
            *sems(0, 0, 0),
            pltpu.SemaphoreType.DMA,
            pltpu.SemaphoreType.DMA((NY,)),
            *sems(0, 0, 0, 0, 0),
            pltpu.SemaphoreType.DMA,
            pltpu.SemaphoreType.DMA((5,)),
        ],
        compiler_params=pltpu.CompilerParams(collective_id=0, has_side_effects=True, vmem_limit_bytes=56 * 2**20),
        name="layer",
    )(features.T, neighbours, self_rows, w_self, w_neigh, cotangent)
    return tuple(
        pl.pallas_call(hand_over, out_shape=outs, in_specs=[VMEM] * 3, out_specs=[VMEM] * 3, name="results")(*got)
    )


def solution(mesh):
    return jax.shard_map(
        on_device,
        mesh=mesh,
        in_specs=(
            P("node", "feat"),
            P("node"),
            P(None, "node"),
            P("feat", None),
            P("feat", None),
            P("node", None),
        ),
        out_specs=(P(("node", "feat"), None), P("feat", None), P("feat", None)),
        check_vma=False,
    )
```

```python
import math

import jax
import jax.numpy as jnp
from jax import lax
from jax.experimental import pallas as pl
from jax.experimental.pallas import tpu as pltpu
from jax.sharding import PartitionSpec as P

NX, NZ, NY = 4, 8, 8
FAN = 10
PAIR = FAN // 2
ROWS = 2048
HALF = ROWS // 2
UNIT = HALF // 2
COLS = 64
WIDE = 2 * COLS
HID = 256
SHARE = 64
TGT = NY * SHARE
GROUP = 2 * NX
NZG = NZ // 2
TAB = GROUP * ROWS
QROW = COLS // NX
NS = 1
RB = SHARE // NS
AT_ONCE = 8
LISTS = NZG * FAN * TGT
MESH = pl.DeviceIdType.MESH
ROOT = math.sqrt(2.0 / math.pi)
BF, F32, I32 = jnp.bfloat16, jnp.float32, jnp.int32


def kernel(
    feat, nb, rows, ws, wn, cot, hidden, gself, gneigh,
    all_nb, my_cot, pieces, tab, wide, nbs, lists, idx, wf, own, theirs, stage, pin, mine, slopes, means, mates,
    gsend, gx, gz, gq,
    s_x, r_x, s_t, r_t, s_h, r_h, s_n, r_n, s_w, r_w, s_f, r_f, s_o, r_o, s_p, r_p, s_s, r_s, s_m, r_m,
    s_gx, r_gx, s_gz, r_gz, s_gq, r_gq, s_idx, s_in,
):
    f_id, n_id = lax.axis_index("feat"), lax.axis_index("node")
    y, c, x, z = f_id // 2, f_id % 2, n_id // NZ, n_id % NZ
    zl, zh = z % 2, z // 2

    def dev(dy, dc, dx, dz):
        core = 1 - c if dc else c
        return {"feat": ((y + dy) % NY) * 2 + core, "node": ((x + dx) % NX) * NZ + (z + dz) % NZ}

    partner = dev(0, 1, 0, 0)
    right, left = dev(0, 0, 1, 0), dev(0, 0, NX - 1, 0)
    over = {"feat": f_id, "node": x * NZ + z + 1 - 2 * zl}

    def remote(src, dst, send, recv, to):
        return pltpu.make_async_remote_copy(
            src_ref=src, dst_ref=dst, send_sem=send, recv_sem=recv, device_id=to, device_id_type=MESH
        )

    def arrived(ref, recv):
        remote(ref, ref, recv, recv, partner).wait_recv()

    def left_here(ref, send):
        remote(ref, ref, send, send, partner).wait_send()

    barrier = pltpu.get_barrier_semaphore()
    friends = [partner]
    friends += [dev(0, 0, 0, d) for d in range(1, NZ)]
    friends += [dev(0, dc, d, 0) for d in range(1, NX) for dc in range(2)]
    friends += [dev(e, 0, 0, 0) for e in range(1, NY)]
    for to in friends:
        pl.semaphore_signal(barrier, inc=1, device_id=to, device_id_type=MESH)

    give = pl.multiple_of((1 - c) * HALF, HALF)
    keep = pl.multiple_of(c * HALF, HALF)
    loads = [
        pltpu.make_async_copy(src, dst, s_in.at[n])
        for n, (src, dst) in enumerate(
            (
                (feat.at[:, pl.ds(keep, HALF)], pieces.at[c]),
                (nb, all_nb),
                (ws, wf.at[f_id, 0]),
                (wn, wf.at[f_id, 1]),
                (cot.at[pl.ds(pl.multiple_of(f_id * SHARE, SHARE), SHARE)], my_cot),
            )
        )
    ]
    for load in loads:
        load.start()

    pl.semaphore_wait(barrier, len(friends))

    swap = remote(feat.at[:, pl.ds(give, HALF)], pieces.at[c], s_x, r_x, partner)
    swap.start()
    loads[0].wait()
    arrived(pieces.at[1 - c], r_x)
    home = x * 2 + zl

    def turn(i, _):
        at = pl.multiple_of(i * 256, 256)
        block = pieces[:, :, pl.ds(at, 256)].reshape(WIDE, 256)
        tab[home, c, pl.ds(at, 256), :] = jnp.transpose(block)
        return 0

    lax.fori_loop(0, HALF // 256, turn, 0)

    xr, xl, far, zo = (x + 1) % NX, (x + NX - 1) % NX, (x + 2) % NX, 1 - zl

    def unit(i, zz, h, core):
        return tab.at[i * 2 + zz, core, pl.ds(h * UNIT, UNIT)]

    def widen(i, zz, h, core):
        base = ((i * 2 + zz) * 2 + core) * HALF + h * UNIT

        def step(k, _):
            at = pl.multiple_of(k * 128, 128)
            piece = tab[i * 2 + zz, core, pl.ds(h * UNIT + at, 128), :]
            wide[pl.ds(pl.multiple_of(base + at, 128), 128), :] = piece.astype(F32)
            return 0

        lax.fori_loop(0, UNIT // 128, step, 0)

    def go(m, i, zz, h, to):
        ref = unit(i, zz, h, c)
        remote(ref, ref, s_t.at[m // 2], r_t.at[m], to).start()

    def passing(i, zz):
        return s_h.at[i * 2 + zz], r_h.at[i * 2 + zz]

    def pass_on(i, zz, h):
        ref = unit(i, zz, h, c)
        send, recv = passing(i, zz)
        remote(ref, ref, send, recv, partner).start()

    def taken(i, zz):
        arrived(tab.at[i * 2 + zz, 1 - c], passing(i, zz)[1])
        for h in range(2):
            widen(i, zz, h, 1 - c)

    def come(m, i, zz, h):
        arrived(unit(i, zz, h, c), r_t.at[m])

    def fetch_own(k, _):
        first = (k // 8) * 128 + c * SHARE + (k % 8) * 8
        for u in range(8):
            own[pl.ds(k * 8 + u, 1), :] = wide[pl.ds(home * ROWS + rows[first + u], 1), :]
        return 0

    go(0, x, zl, 0, right)
    go(3, x, zl, 1, left)
    go(4, x, zl, 0, over)
    pass_on(x, zl, 0)
    pass_on(x, zl, 1)

    loads[1].wait()
    cuts = []
    for b in range(NY):
        lo = all_nb[:, b * 128 : b * 128 + 64]
        hi = all_nb[:, b * 128 + 64 : b * 128 + 128]
        cuts.append(jnp.where(c == 0, lo, hi))
    named = jnp.concatenate(cuts, axis=1)
    nbs[zh] = named[:PAIR] | (named[PAIR:] << 16)
    widen(x, zl, 0, c)
    widen(x, zl, 1, c)
    taken(x, zl)
    go(1, x, zl, 1, right)
    go(2, x, zl, 0, left)
    go(5, x, zl, 1, over)
    loads[2].wait()
    loads[3].wait()
    loads[4].wait()
    for d in range(1, NY):
        remote(wf.at[f_id], wf.at[f_id], s_w, r_w, dev(d, 0, 0, 0)).start()
    remote(wf.at[f_id], wf.at[f_id], s_f, r_f, partner).start()

    lax.fori_loop(0, TGT // 8, fetch_own, 0)
    mates[...] = own[...].astype(BF).reshape(NY, SHARE, WIDE)
    theirs[y] = mates[y]
    for e in range(1, NY):
        remote(mates.at[(y + e) % NY], theirs.at[y], s_o, r_o, dev(e, 0, 0, 0)).start()

    come(0, xl, zl, 0)
    go(6, xl, zl, 0, right)
    go(11, xl, zl, 0, over)
    come(3, xr, zl, 1)
    go(7, xr, zl, 1, left)
    go(12, xr, zl, 1, over)
    come(4, x, zo, 0)
    go(8, x, zo, 0, dev(0, 0, 2, 0))
    go(10, x, zo, 0, left)
    pass_on(xl, zl, 0)
    pass_on(xr, zl, 1)
    pass_on(x, zo, 0)
    for d in range(1, NZG):
        remote(nbs.at[zh], nbs.at[zh], s_n.at[d], r_n.at[d], dev(0, 0, 0, 2 * d)).start()
    widen(xl, zl, 0, c)
    widen(xr, zl, 1, c)
    come(1, xl, zl, 1)
    go(13, xl, zl, 1, over)
    come(5, x, zo, 1)
    go(9, x, zo, 1, dev(0, 0, 2, 0))
    come(2, xr, zl, 0)
    pass_on(xl, zl, 1)
    pass_on(xr, zl, 0)
    pass_on(x, zo, 1)
    widen(x, zo, 0, c)
    widen(xl, zl, 1, c)
    widen(xr, zl, 0, c)
    widen(x, zo, 1, c)
    come(6, far, zl, 0)
    pass_on(far, zl, 0)
    come(7, far, zl, 1)
    pass_on(far, zl, 1)
    widen(far, zl, 0, c)
    widen(far, zl, 1, c)

    for d in range(1, NZG):
        at = (zh + NZG - d) % NZG
        arrived(nbs.at[at], r_n.at[d])
    for g in range(NZG):
        words = nbs[g]
        for h, n in enumerate((words & 0xFFFF, (words >> 16) & 0xFFFF)):
            part_of = n >> 11
            inside = ((part_of & 7) >> 1) == zh
            row = ((((part_of >> 3) << 1) | (part_of & 1)) << 11) | (n & (ROWS - 1))
            lists[g, h * PAIR : (h + 1) * PAIR, :] = jnp.where(inside, row, TAB)
    to_scalar = [
        pltpu.make_async_copy(lists.at[g, f], idx.at[pl.ds((g * FAN + f) * TGT, TGT)], s_idx)
        for g in range(NZG)
        for f in range(FAN)
    ]
    for copy in to_scalar:
        copy.start()
    rest = ((11, xl, 0), (12, xr, 1), (10, xr, 0), (8, far, 0), (13, xl, 1), (9, far, 1))
    for m, i, h in rest:
        come(m, i, zo, h)
        pass_on(i, zo, h)
    for m, i, h in rest:
        widen(i, zo, h, c)
    for i, zz in ((xl, zl), (xr, zl), (x, zo), (far, zl), (xr, zo), (xl, zo), (far, zo)):
        taken(i, zz)
    wide[pl.ds(TAB, 8), :] = jnp.zeros((8, WIDE), F32)
    pltpu.make_async_copy(idx, idx, s_idx).wait()

    def total_of(g, b, s):
        start = g * (FAN * TGT) + b * SHARE + s * RB

        def some(k, _):
            first = start + k * AT_ONCE
            for u in range(AT_ONCE):
                total = None
                for f in range(FAN):
                    skip = f * TGT + u
                    row = wide[pl.ds(idx.at[pl.ds(skip, LISTS - skip)][first], 1), :]
                    total = row if total is None else total + row
                own[pl.ds(k * AT_ONCE + u, 1), :] = total
            return 0

        lax.fori_loop(0, RB // AT_ONCE, some, 0)

    def plane(s, d):
        g = (zh + d) % NZG

        def one(e, _):
            total_of(g, (y + e) % NY, s)
            stage[e, d - 1] = own[pl.ds(0, RB), :].astype(BF)
            remote(stage.at[e, d - 1], pin.at[e, d - 1], s_p, r_p.at[e], dev(0, 0, 0, 2 * d)).start()
            return 0

        lax.fori_loop(0, NY, one, 0)

    def finish(s, e):
        b = (y + e) % NY
        total_of(zh, b, s)
        total = own[pl.ds(0, RB), :]
        arrived(pin.at[e], r_p.at[e])
        for d in range(NZG - 1):
            total = total + pin[e, d].astype(F32)
        means[s, b] = (total * (1.0 / FAN)).astype(BF)

    def home_plane(s):
        def one(e, _):
            finish(s, e)
            remote(means.at[s, (y + e) % NY], mine.at[s, y], s_m, r_m, dev(e, 0, 0, 0)).start()
            return 0

        lax.fori_loop(1, NY, one, 0)
        finish(s, 0)
        mine[s, y] = means[s, y]

    def activate(s):
        pre = jnp.zeros((RB, HID), F32)
        for b in range(NY):
            w_own = jnp.concatenate([wf[2 * b, 0], wf[2 * b + 1, 0]], axis=0)
            pre = pre + jnp.dot(theirs[b, s * RB : (s + 1) * RB, :], w_own, preferred_element_type=F32)
        for e in range(NY):
            src = (y + NY - e) % NY
            w_mean = jnp.concatenate([wf[2 * src, 1], wf[2 * src + 1, 1]], axis=0)
            if e == 0:
                arrived(mine.at[s, pl.ds(0, NY - 1)], r_m)
            pre = pre + jnp.dot(mine[s, src], w_mean, preferred_element_type=F32)
        square = pre * pre
        th = jnp.tanh(ROOT * (pre + 0.044715 * (square * pre)))
        half = 0.5 * (1.0 + th)
        dydx = half + 0.5 * pre * (1.0 - th * th) * (ROOT * (1.0 + 3.0 * 0.044715 * square))
        slopes[s, y] = (my_cot[s * RB : (s + 1) * RB, :].astype(F32) * dydx).astype(BF)
        for e in range(1, NY):
            remote(slopes.at[s, y], slopes.at[s, y], s_s, r_s, dev(e, 0, 0, 0)).start()
        hidden[s * RB : (s + 1) * RB, :] = (pre * half).astype(BF)

    def grads(s):
        mates_turned = jnp.transpose(mates[:, s * RB : (s + 1) * RB, :].reshape(NY * RB, WIDE))
        means_turned = jnp.transpose(means[s].reshape(NY * RB, WIDE))
        arrived(slopes.at[s, pl.ds(0, NY - 1)], r_s)
        slope = slopes[s].reshape(NY * RB, HID)
        return [jnp.dot(t, slope, preferred_element_type=F32) for t in (mates_turned, means_turned)]

    plane(0, 2)
    plane(0, 1)
    arrived(wf.at[pl.ds(0, NY - 1)], r_w)
    for d in range(1, NY):
        at = ((y + NY - d) % NY) * 2 + c
        remote(wf.at[at], wf.at[at], s_f, r_f, partner).start()
    plane(0, 3)
    home_plane(0)
    arrived(wf.at[pl.ds(0, NY)], r_f)
    arrived(theirs.at[pl.ds(0, NY - 1)], r_o)
    activate(0)
    both = grads(0)

    for p in range(2):
        for q in range(NX):
            for w in range(2):
                at = p * COLS + q * QROW
                gsend[p * NX + q, w] = both[w][at : at + QROW].astype(BF)
    hops = [(dc, dx) for dx in range(NX) for dc in range(2) if dc or dx]
    for n, (dc, dx) in enumerate(hops):
        core = 1 - c if dc else c
        remote(gsend.at[core * NX + (x + dx) % NX], gx.at[n], s_gx, r_gx, dev(0, dc, dx, 0)).start()
    total = gsend[c * NX + x].astype(F32)
    arrived(gx, r_gx)
    for n in range(len(hops)):
        total = total + gx[n].astype(F32)
    gz[z] = total.astype(BF)
    for d in range(1, NZ):
        remote(gz.at[z], gz.at[z], s_gz, r_gz, dev(0, 0, 0, d)).start()
    arrived(gz.at[pl.ds(0, NZ - 1)], r_gz)
    total = gz[0].astype(F32)
    for d in range(1, NZ):
        total = total + gz[d].astype(F32)
    gq[x] = total
    for d in range(1, NX):
        remote(gq.at[x], gq.at[x], s_gq, r_gq, dev(0, 0, d, 0)).start()
    arrived(gq.at[pl.ds(0, NX - 1)], r_gq)
    for q in range(NX):
        gself[q * QROW : (q + 1) * QROW, :] = gq[q, 0]
        gneigh[q * QROW : (q + 1) * QROW, :] = gq[q, 1]

    left_here(feat.at[:, pl.ds(give, HALF)], s_x)
    for m in range(7):
        left_here(tab.at[home, c], s_t.at[m])
    for m in range(GROUP):
        left_here(tab.at[home, c], s_h.at[m])
    for d in range(1, NZG):
        left_here(nbs.at[zh], s_n.at[d])
    left_here(wf.at[pl.ds(0, NY - 1)], s_w)
    left_here(theirs.at[pl.ds(0, NY - 1)], s_o)
    left_here(wf.at[pl.ds(0, NY)], s_f)

    left_here(stage, s_p)
    left_here(mine.at[0, pl.ds(0, NY - 1)], s_m)
    left_here(slopes.at[0, pl.ds(0, NY - 1)], s_s)
    left_here(gx, s_gx)
    left_here(gz.at[pl.ds(0, NZ - 1)], s_gz)
    left_here(gq.at[pl.ds(0, NX - 1)], s_gq)


def hand_over(a, b, c, out_a, out_b, out_c):
    out_a[...] = a[...]
    out_b[...] = b[...]
    out_c[...] = c[...]


VMEM = pl.BlockSpec(memory_space=pltpu.VMEM)
SMEM = pl.BlockSpec(memory_space=pltpu.SMEM)
HBM = pl.BlockSpec(memory_space=pl.ANY)


def sems(*counts):
    return [pltpu.SemaphoreType.DMA((n,)) if n else pltpu.SemaphoreType.DMA for n in counts for _ in range(2)]


def on_device(features, self_rows, neighbours, w_self, w_neigh, cotangent):
    shape = jax.ShapeDtypeStruct
    outs = [shape((SHARE, HID), BF), shape((COLS, HID), F32), shape((COLS, HID), F32)]
    got = pl.pallas_call(
        kernel,
        out_shape=outs,
        in_specs=[HBM, HBM, SMEM, HBM, HBM, HBM],
        out_specs=[VMEM] * 3,
        scratch_shapes=[
            pltpu.VMEM((FAN, 2 * TGT), I32),
            pltpu.VMEM((SHARE, HID), BF),
            pltpu.VMEM((2, COLS, HALF), BF),
            pltpu.VMEM((GROUP, 2, HALF, WIDE), BF),
            pltpu.VMEM((TAB + 8, WIDE), F32),
            pltpu.VMEM((NZG, PAIR, TGT), I32),
            pltpu.VMEM((NZG, FAN, TGT), I32),
            pltpu.SMEM((LISTS,), I32),
            pltpu.VMEM((2 * NY, 2, COLS, HID), BF),
            pltpu.VMEM((TGT, WIDE), F32),
            pltpu.VMEM((NY, SHARE, WIDE), BF),
            pltpu.VMEM((NY, NZG - 1, RB, WIDE), BF),
            pltpu.VMEM((NY, NZG - 1, RB, WIDE), BF),
            pltpu.VMEM((NS, NY, RB, WIDE), BF),
            pltpu.VMEM((NS, NY, RB, HID), BF),
            pltpu.VMEM((NS, NY, RB, WIDE), BF),
            pltpu.VMEM((NY, SHARE, WIDE), BF),
            pltpu.VMEM((2 * NX, 2, QROW, HID), BF),
            pltpu.VMEM((2 * NX - 1, 2, QROW, HID), BF),
            pltpu.VMEM((NZ, 2, QROW, HID), BF),
            pltpu.VMEM((NX, 2, QROW, HID), F32),
            *sems(0),
            *(pltpu.SemaphoreType.DMA((n,)) for n in (7, 14, GROUP, GROUP, NZG, NZG)),
            *sems(0, 0, 0),
            pltpu.SemaphoreType.DMA,
            pltpu.SemaphoreType.DMA((NY,)),
            *sems(0, 0, 0, 0, 0),
            pltpu.SemaphoreType.DMA,
            pltpu.SemaphoreType.DMA((5,)),
        ],
        compiler_params=pltpu.CompilerParams(collective_id=0, has_side_effects=True, vmem_limit_bytes=56 * 2**20),
        name="layer",
    )(features.T, neighbours, self_rows, w_self, w_neigh, cotangent)
    return tuple(
        pl.pallas_call(hand_over, out_shape=outs, in_specs=[VMEM] * 3, out_specs=[VMEM] * 3, name="results")(*got)
    )


def solution(mesh):
    return jax.shard_map(
        on_device,
        mesh=mesh,
        in_specs=(
            P("node", "feat"),
            P("node"),
            P(None, "node"),
            P("feat", None),
            P("feat", None),
            P("node", None),
        ),
        out_specs=(P(("node", "feat"), None), P("feat", None), P("feat", None)),
        check_vma=False,
    )
```

```python
import math

import jax
import jax.numpy as jnp
from jax import lax
from jax.experimental import pallas as pl
from jax.experimental.pallas import tpu as pltpu
from jax.sharding import PartitionSpec as P

NX, NZ, NY = 4, 8, 8
FAN = 10
PAIR = FAN // 2
ROWS = 2048
HALF = ROWS // 2
UNIT = HALF // 2
COLS = 64
WIDE = 2 * COLS
HID = 256
SHARE = 64
TGT = NY * SHARE
GROUP = 2 * NX
NZG = NZ // 2
TAB = GROUP * ROWS
QROW = COLS // NX
NS = 1
RB = SHARE // NS
AT_ONCE = 8
LISTS = NZG * FAN * TGT
MESH = pl.DeviceIdType.MESH
ROOT = math.sqrt(2.0 / math.pi)
BF, F32, I32 = jnp.bfloat16, jnp.float32, jnp.int32


def kernel(
    feat, nb, rows, ws, wn, cot, hidden, gself, gneigh,
    all_nb, my_cot, pieces, tab, wide, nbs, lists, idx, wf, own, theirs, stage, pin, mine, slopes, means, mates,
    gsend, gx, gz, gq,
    s_x, r_x, s_t, r_t, s_h, r_h, s_n, r_n, s_w, r_w, s_f, r_f, s_o, r_o, s_p, r_p, s_s, r_s, s_m, r_m,
    s_gx, r_gx, s_gz, r_gz, s_gq, r_gq, s_idx, s_in,
):
    f_id, n_id = lax.axis_index("feat"), lax.axis_index("node")
    y, c, x, z = f_id // 2, f_id % 2, n_id // NZ, n_id % NZ
    zl, zh = z % 2, z // 2

    def dev(dy, dc, dx, dz):
        core = 1 - c if dc else c
        return {"feat": ((y + dy) % NY) * 2 + core, "node": ((x + dx) % NX) * NZ + (z + dz) % NZ}

    partner = dev(0, 1, 0, 0)
    right, left = dev(0, 0, 1, 0), dev(0, 0, NX - 1, 0)
    over = {"feat": f_id, "node": x * NZ + z + 1 - 2 * zl}

    def remote(src, dst, send, recv, to):
        return pltpu.make_async_remote_copy(
            src_ref=src, dst_ref=dst, send_sem=send, recv_sem=recv, device_id=to, device_id_type=MESH
        )

    def arrived(ref, recv):
        remote(ref, ref, recv, recv, partner).wait_recv()

    def left_here(ref, send):
        remote(ref, ref, send, send, partner).wait_send()

    barrier = pltpu.get_barrier_semaphore()
    friends = [partner]
    friends += [dev(0, 0, 0, d) for d in range(1, NZ)]
    friends += [dev(0, dc, d, 0) for d in range(1, NX) for dc in range(2)]
    friends += [dev(e, 0, 0, 0) for e in range(1, NY)]
    for to in friends:
        pl.semaphore_signal(barrier, inc=1, device_id=to, device_id_type=MESH)

    give = pl.multiple_of((1 - c) * HALF, HALF)
    keep = pl.multiple_of(c * HALF, HALF)
    loads = [
        pltpu.make_async_copy(src, dst, s_in.at[n])
        for n, (src, dst) in enumerate(
            (
                (feat.at[:, pl.ds(keep, HALF)], pieces.at[c]),
                (nb, all_nb),
                (ws, wf.at[f_id, 0]),
                (wn, wf.at[f_id, 1]),
                (cot.at[pl.ds(pl.multiple_of(f_id * SHARE, SHARE), SHARE)], my_cot),
            )
        )
    ]
    for load in loads:
        load.start()

    pl.semaphore_wait(barrier, len(friends))

    swap = remote(feat.at[:, pl.ds(give, HALF)], pieces.at[c], s_x, r_x, partner)
    swap.start()
    loads[0].wait()
    arrived(pieces.at[1 - c], r_x)
    home = x * 2 + zl

    def turn(i, _):
        at = pl.multiple_of(i * 256, 256)
        block = pieces[:, :, pl.ds(at, 256)].reshape(WIDE, 256)
        tab[home, c, pl.ds(at, 256), :] = jnp.transpose(block)
        return 0

    lax.fori_loop(0, HALF // 256, turn, 0)

    xr, xl, far, zo = (x + 1) % NX, (x + NX - 1) % NX, (x + 2) % NX, 1 - zl

    def unit(i, zz, h, core):
        return tab.at[i * 2 + zz, core, pl.ds(h * UNIT, UNIT)]

    def widen(i, zz, h, core):
        base = ((i * 2 + zz) * 2 + core) * HALF + h * UNIT

        def step(k, _):
            at = pl.multiple_of(k * 128, 128)
            piece = tab[i * 2 + zz, core, pl.ds(h * UNIT + at, 128), :]
            wide[pl.ds(pl.multiple_of(base + at, 128), 128), :] = piece.astype(F32)
            return 0

        lax.fori_loop(0, UNIT // 128, step, 0)

    def go(m, i, zz, h, to):
        ref = unit(i, zz, h, c)
        remote(ref, ref, s_t.at[m // 2], r_t.at[m], to).start()

    def passing(i, zz):
        return s_h.at[i * 2 + zz], r_h.at[i * 2 + zz]

    def pass_on(i, zz, h):
        ref = unit(i, zz, h, c)
        send, recv = passing(i, zz)
        remote(ref, ref, send, recv, partner).start()

    def taken(i, zz):
        arrived(tab.at[i * 2 + zz, 1 - c], passing(i, zz)[1])
        for h in range(2):
            widen(i, zz, h, 1 - c)

    def come(m, i, zz, h):
        arrived(unit(i, zz, h, c), r_t.at[m])

    def fetch_own(k, _):
        first = (k // 8) * 128 + c * SHARE + (k % 8) * 8
        for u in range(8):
            own[pl.ds(k * 8 + u, 1), :] = wide[pl.ds(home * ROWS + rows[first + u], 1), :]
        return 0

    go(0, x, zl, 0, right)
    go(3, x, zl, 1, left)
    go(4, x, zl, 0, over)
    pass_on(x, zl, 0)
    pass_on(x, zl, 1)

    loads[1].wait()
    cuts = []
    for b in range(NY):
        lo = all_nb[:, b * 128 : b * 128 + 64]
        hi = all_nb[:, b * 128 + 64 : b * 128 + 128]
        cuts.append(jnp.where(c == 0, lo, hi))
    named = jnp.concatenate(cuts, axis=1)
    nbs[zh] = named[:PAIR] | (named[PAIR:] << 16)
    widen(x, zl, 0, c)
    widen(x, zl, 1, c)
    taken(x, zl)
    go(1, x, zl, 1, right)
    go(2, x, zl, 0, left)
    go(5, x, zl, 1, over)
    loads[2].wait()
    loads[3].wait()
    loads[4].wait()
    for d in range(1, NY):
        remote(wf.at[f_id], wf.at[f_id], s_w, r_w, dev(d, 0, 0, 0)).start()
    remote(wf.at[f_id], wf.at[f_id], s_f, r_f, partner).start()

    lax.fori_loop(0, TGT // 8, fetch_own, 0)
    mates[...] = own[...].astype(BF).reshape(NY, SHARE, WIDE)
    theirs[y] = mates[y]
    for e in range(1, NY):
        remote(mates.at[(y + e) % NY], theirs.at[y], s_o, r_o, dev(e, 0, 0, 0)).start()

    come(0, xl, zl, 0)
    go(6, xl, zl, 0, right)
    go(11, xl, zl, 0, over)
    come(3, xr, zl, 1)
    go(7, xr, zl, 1, left)
    go(12, xr, zl, 1, over)
    come(4, x, zo, 0)
    go(8, x, zo, 0, dev(0, 0, 2, 0))
    go(10, x, zo, 0, left)
    pass_on(xl, zl, 0)
    pass_on(xr, zl, 1)
    pass_on(x, zo, 0)
    for d in range(1, NZG):
        remote(nbs.at[zh], nbs.at[zh], s_n.at[d], r_n.at[d], dev(0, 0, 0, 2 * d)).start()
    widen(xl, zl, 0, c)
    widen(xr, zl, 1, c)
    come(1, xl, zl, 1)
    go(13, xl, zl, 1, over)
    come(5, x, zo, 1)
    go(9, x, zo, 1, dev(0, 0, 2, 0))
    come(2, xr, zl, 0)
    pass_on(xl, zl, 1)
    pass_on(xr, zl, 0)
    pass_on(x, zo, 1)
    widen(x, zo, 0, c)
    widen(xl, zl, 1, c)
    widen(xr, zl, 0, c)
    widen(x, zo, 1, c)
    come(6, far, zl, 0)
    pass_on(far, zl, 0)
    come(7, far, zl, 1)
    pass_on(far, zl, 1)
    widen(far, zl, 0, c)
    widen(far, zl, 1, c)

    for d in range(1, NZG):
        at = (zh + NZG - d) % NZG
        arrived(nbs.at[at], r_n.at[d])
    for g in range(NZG):
        words = nbs[g]
        for h, n in enumerate((words & 0xFFFF, (words >> 16) & 0xFFFF)):
            part_of = n >> 11
            inside = ((part_of & 7) >> 1) == zh
            row = ((((part_of >> 3) << 1) | (part_of & 1)) << 11) | (n & (ROWS - 1))
            lists[g, h * PAIR : (h + 1) * PAIR, :] = jnp.where(inside, row, TAB)
    to_scalar = [
        pltpu.make_async_copy(lists.at[g, f], idx.at[pl.ds((g * FAN + f) * TGT, TGT)], s_idx)
        for g in range(NZG)
        for f in range(FAN)
    ]
    for copy in to_scalar:
        copy.start()
    rest = ((11, xl, 0), (12, xr, 1), (10, xr, 0), (8, far, 0), (13, xl, 1), (9, far, 1))
    for m, i, h in rest:
        come(m, i, zo, h)
        pass_on(i, zo, h)
    for m, i, h in rest:
        widen(i, zo, h, c)
    for i, zz in ((xl, zl), (xr, zl), (x, zo), (far, zl), (xr, zo), (xl, zo), (far, zo)):
        taken(i, zz)
    wide[pl.ds(TAB, 8), :] = jnp.zeros((8, WIDE), F32)
    pltpu.make_async_copy(idx, idx, s_idx).wait()

    def total_of(g, b, s):
        start = g * (FAN * TGT) + b * SHARE + s * RB

        def some(k, _):
            first = start + k * AT_ONCE
            for u in range(AT_ONCE):
                total = None
                for f in range(FAN):
                    skip = f * TGT + u
                    row = wide[pl.ds(idx.at[pl.ds(skip, LISTS - skip)][first], 1), :]
                    total = row if total is None else total + row
                own[pl.ds(k * AT_ONCE + u, 1), :] = total
            return 0

        lax.fori_loop(0, RB // AT_ONCE, some, 0)

    def plane(s, d):
        g = (zh + d) % NZG

        def one(e, _):
            total_of(g, (y + e) % NY, s)
            stage[e, d - 1] = own[pl.ds(0, RB), :].astype(BF)
            remote(stage.at[e, d - 1], pin.at[e, d - 1], s_p, r_p.at[e], dev(0, 0, 0, 2 * d)).start()
            return 0

        lax.fori_loop(0, NY, one, 0)

    def finish(s, e):
        b = (y + e) % NY
        total_of(zh, b, s)
        total = own[pl.ds(0, RB), :]
        arrived(pin.at[e], r_p.at[e])
        for d in range(NZG - 1):
            total = total + pin[e, d].astype(F32)
        means[s, b] = (total * (1.0 / FAN)).astype(BF)

    def home_plane(s):
        def one(e, _):
            finish(s, e)
            remote(means.at[s, (y + e) % NY], mine.at[s, y], s_m, r_m, dev(e, 0, 0, 0)).start()
            return 0

        lax.fori_loop(1, NY, one, 0)
        finish(s, 0)
        mine[s, y] = means[s, y]

    def activate(s):
        pre = jnp.zeros((RB, HID), F32)
        for b in range(0, NY, 2):
            w_own = jnp.concatenate([wf[2 * b + k, 0] for k in range(4)], axis=0)
            got = jnp.concatenate([theirs[b], theirs[b + 1]], axis=1)
            pre = pre + jnp.dot(got, w_own, preferred_element_type=F32)
        arrived(mine.at[s, pl.ds(0, NY - 1)], r_m)
        for b in range(0, NY, 2):
            w_mean = jnp.concatenate([wf[2 * b + k, 1] for k in range(4)], axis=0)
            got = jnp.concatenate([mine[s, b], mine[s, b + 1]], axis=1)
            pre = pre + jnp.dot(got, w_mean, preferred_element_type=F32)
        square = pre * pre
        th = jnp.tanh(ROOT * (pre + 0.044715 * (square * pre)))
        half = 0.5 * (1.0 + th)
        dydx = half + 0.5 * pre * (1.0 - th * th) * (ROOT * (1.0 + 3.0 * 0.044715 * square))
        slopes[s, y] = (my_cot[s * RB : (s + 1) * RB, :].astype(F32) * dydx).astype(BF)
        for e in range(1, NY):
            remote(slopes.at[s, y], slopes.at[s, y], s_s, r_s, dev(e, 0, 0, 0)).start()
        hidden[s * RB : (s + 1) * RB, :] = (pre * half).astype(BF)

    def grads(s):
        mates_turned = jnp.transpose(mates[:, s * RB : (s + 1) * RB, :].reshape(NY * RB, WIDE))
        means_turned = jnp.transpose(means[s].reshape(NY * RB, WIDE))
        arrived(slopes.at[s, pl.ds(0, NY - 1)], r_s)
        slope = slopes[s].reshape(NY * RB, HID)
        return [jnp.dot(t, slope, preferred_element_type=F32) for t in (mates_turned, means_turned)]

    plane(0, 2)
    plane(0, 1)
    arrived(wf.at[pl.ds(0, NY - 1)], r_w)
    for d in range(1, NY):
        at = ((y + NY - d) % NY) * 2 + c
        remote(wf.at[at], wf.at[at], s_f, r_f, partner).start()
    plane(0, 3)
    home_plane(0)
    arrived(wf.at[pl.ds(0, NY)], r_f)
    arrived(theirs.at[pl.ds(0, NY - 1)], r_o)
    activate(0)
    both = grads(0)

    for p in range(2):
        for q in range(NX):
            for w in range(2):
                at = p * COLS + q * QROW
                gsend[p * NX + q, w] = both[w][at : at + QROW].astype(BF)
    hops = [(dc, dx) for dx in range(NX) for dc in range(2) if dc or dx]
    for n, (dc, dx) in enumerate(hops):
        core = 1 - c if dc else c
        remote(gsend.at[core * NX + (x + dx) % NX], gx.at[n], s_gx, r_gx, dev(0, dc, dx, 0)).start()
    total = gsend[c * NX + x].astype(F32)
    arrived(gx, r_gx)
    for n in range(len(hops)):
        total = total + gx[n].astype(F32)
    gz[z] = total.astype(BF)
    for d in range(1, NZ):
        remote(gz.at[z], gz.at[z], s_gz, r_gz, dev(0, 0, 0, d)).start()
    arrived(gz.at[pl.ds(0, NZ - 1)], r_gz)
    total = gz[0].astype(F32)
    for d in range(1, NZ):
        total = total + gz[d].astype(F32)
    gq[x] = total
    for d in range(1, NX):
        remote(gq.at[x], gq.at[x], s_gq, r_gq, dev(0, 0, d, 0)).start()
    arrived(gq.at[pl.ds(0, NX - 1)], r_gq)
    for q in range(NX):
        gself[q * QROW : (q + 1) * QROW, :] = gq[q, 0]
        gneigh[q * QROW : (q + 1) * QROW, :] = gq[q, 1]

    left_here(feat.at[:, pl.ds(give, HALF)], s_x)
    for m in range(7):
        left_here(tab.at[home, c], s_t.at[m])
    for m in range(GROUP):
        left_here(tab.at[home, c], s_h.at[m])
    for d in range(1, NZG):
        left_here(nbs.at[zh], s_n.at[d])
    left_here(wf.at[pl.ds(0, NY - 1)], s_w)
    left_here(theirs.at[pl.ds(0, NY - 1)], s_o)
    left_here(wf.at[pl.ds(0, NY)], s_f)

    left_here(stage, s_p)
    left_here(mine.at[0, pl.ds(0, NY - 1)], s_m)
    left_here(slopes.at[0, pl.ds(0, NY - 1)], s_s)
    left_here(gx, s_gx)
    left_here(gz.at[pl.ds(0, NZ - 1)], s_gz)
    left_here(gq.at[pl.ds(0, NX - 1)], s_gq)


def hand_over(a, b, c, out_a, out_b, out_c):
    out_a[...] = a[...]
    out_b[...] = b[...]
    out_c[...] = c[...]


VMEM = pl.BlockSpec(memory_space=pltpu.VMEM)
SMEM = pl.BlockSpec(memory_space=pltpu.SMEM)
HBM = pl.BlockSpec(memory_space=pl.ANY)


def sems(*counts):
    return [pltpu.SemaphoreType.DMA((n,)) if n else pltpu.SemaphoreType.DMA for n in counts for _ in range(2)]


def on_device(features, self_rows, neighbours, w_self, w_neigh, cotangent):
    shape = jax.ShapeDtypeStruct
    outs = [shape((SHARE, HID), BF), shape((COLS, HID), F32), shape((COLS, HID), F32)]
    got = pl.pallas_call(
        kernel,
        out_shape=outs,
        in_specs=[HBM, HBM, SMEM, HBM, HBM, HBM],
        out_specs=[VMEM] * 3,
        scratch_shapes=[
            pltpu.VMEM((FAN, 2 * TGT), I32),
            pltpu.VMEM((SHARE, HID), BF),
            pltpu.VMEM((2, COLS, HALF), BF),
            pltpu.VMEM((GROUP, 2, HALF, WIDE), BF),
            pltpu.VMEM((TAB + 8, WIDE), F32),
            pltpu.VMEM((NZG, PAIR, TGT), I32),
            pltpu.VMEM((NZG, FAN, TGT), I32),
            pltpu.SMEM((LISTS,), I32),
            pltpu.VMEM((2 * NY, 2, COLS, HID), BF),
            pltpu.VMEM((TGT, WIDE), F32),
            pltpu.VMEM((NY, SHARE, WIDE), BF),
            pltpu.VMEM((NY, NZG - 1, RB, WIDE), BF),
            pltpu.VMEM((NY, NZG - 1, RB, WIDE), BF),
            pltpu.VMEM((NS, NY, RB, WIDE), BF),
            pltpu.VMEM((NS, NY, RB, HID), BF),
            pltpu.VMEM((NS, NY, RB, WIDE), BF),
            pltpu.VMEM((NY, SHARE, WIDE), BF),
            pltpu.VMEM((2 * NX, 2, QROW, HID), BF),
            pltpu.VMEM((2 * NX - 1, 2, QROW, HID), BF),
            pltpu.VMEM((NZ, 2, QROW, HID), BF),
            pltpu.VMEM((NX, 2, QROW, HID), F32),
            *sems(0),
            *(pltpu.SemaphoreType.DMA((n,)) for n in (7, 14, GROUP, GROUP, NZG, NZG)),
            *sems(0, 0, 0),
            pltpu.SemaphoreType.DMA,
            pltpu.SemaphoreType.DMA((NY,)),
            *sems(0, 0, 0, 0, 0),
            pltpu.SemaphoreType.DMA,
            pltpu.SemaphoreType.DMA((5,)),
        ],
        compiler_params=pltpu.CompilerParams(collective_id=0, has_side_effects=True, vmem_limit_bytes=56 * 2**20),
        name="layer",
    )(features.T, neighbours, self_rows, w_self, w_neigh, cotangent)
    return tuple(
        pl.pallas_call(hand_over, out_shape=outs, in_specs=[VMEM] * 3, out_specs=[VMEM] * 3, name="results")(*got)
    )


def solution(mesh):
    return jax.shard_map(
        on_device,
        mesh=mesh,
        in_specs=(
            P("node", "feat"),
            P("node"),
            P(None, "node"),
            P("feat", None),
            P("feat", None),
            P("node", None),
        ),
        out_specs=(P(("node", "feat"), None), P("feat", None), P("feat", None)),
        check_vma=False,
    )
```
